128 devices in a mesh: dp: 16 (over z_lo, x, core), mp: 8 (over y, z_hi).
Axes of the slice: x: 4, y: 4, z: 4 (z_hi: 2, z_lo: 2; z = z_hi * 2 + z_lo), core: 2. Of those that a mesh axis runs over, the one named last changes fastest.
Arguments:
- hidden: bfloat16 [8192, 4096], P('dp'), may hold values from -6 to 6
- segment_ids: int32 [16, 512], P('dp'), may hold values from 0 to 15, never falling along the last dimension, each value on 1 to 128 neighbouring positions
- attn_gain: float32 [4096], replicated, may hold values from 0.25 to 1.75
- w_query: bfloat16 [4096, 4096], P(None, 'mp'), as said below
- w_key: bfloat16 [4096, 1024], P(None, 'mp'), as said below
- w_value: bfloat16 [4096, 1024], P(None, 'mp'), may hold values from -0.09375 to 0.09375
- w_out: bfloat16 [4096, 4096], P('mp'), may hold values from -0.09375 to 0.09375
- final_gain: float32 [4096], replicated, may hold values from 0.25 to 1.75
- adapter: bfloat16 [4096, 1024], replicated, may hold values from -0.09375 to 0.09375
- features: bfloat16 [256, 1024], P(('dp', 'mp')), may hold values from -6 to 6
- ln_gain: float32 [1024], replicated, may hold values from 0.25 to 1.75
- ln_bias: float32 [1024], replicated, may hold values from -3 to 3
- pair_ids: int32 [256], replicated, may hold values from 0 to 255, each once
Outputs:
- loss: float32 [], replicated
- adapter_grad: float32 [4096, 1024], P(('dp', 'mp'))
- feature_grad: float32 [256, 1024], P(('dp', 'mp'))
The draws below stay inside these ranges and needn't reach their ends.
Inputs may be any that keep to these rules, and one draw needn't show every extreme that they name: `segment_ids`: within each row segment ids never fall; each of the 16 ids has 1 to 128 tokens and one has exactly 128. `pair_ids`: each text is paired with exactly one image. `w_query`: independent entries of mean zero and deviation about 4096^(-1/2). `w_key`: entries of mean zero.
All inputs are finite; a program needn't handle non-finite values.
Results may differ from the reference program's by a relative error of at most 0.02.
Values may be sent and summed in bfloat16 or wider, within the bound.
No kernel may reach another device: no remote copies, remote signals or barrier semaphores. Data moves between devices by JAX's collectives and lax.ppermute only.
A program may use at most 128 MiB of HBM per device.

```python
import math
import jax
import jax.numpy as jnp
import numpy as np
from jax import lax

D = 4096
H = 32
KVH = 8
HD = 128
E = 1024
TOK_DEV = 512
DOCS_DEV = 16
DOC_MOST = 128
TOKENS = 8192
B = 256
N_DP = 16
N_MP = 8


def shared_columns(key):
    return jax.random.truncated_normal(key, -6.0, 6.0, (D, H * HD), jnp.float32) * D ** (-0.5)


def draw_w_query(key, part):
    base = shared_columns(key)
    return base.astype(jnp.bfloat16)


def draw_w_key(key, part):
    key = jax.random.fold_in(key, 9)
    return (jax.random.truncated_normal(key, -6.0, 6.0, (D, KVH * HD), jnp.float32) * D ** (-0.5)).astype(jnp.bfloat16)


def block_scale(key, extent, shards, low, top_value):
    def one(axis_at, shards_of):
        draws = jax.random.uniform(jax.random.fold_in(jax.random.fold_in(key, 6), axis_at), (shards_of,), jnp.float32, low / len(shards), top_value / len(shards))
        return jnp.repeat(jnp.exp(draws), extent[axis_at] // shards_of).reshape((-1,) + (1,) * (len(extent) - axis_at - 1))

    level = one(*shards[0])
    for cut in shards[1:]:
        level = level * one(*cut)
    return level


def profile(number_of, total, reach, slope):
    loads = [(1 << 20) // math.isqrt(rank ** slope) + 1 for rank in range(2, number_of + 1)]
    spare, given = total - reach - (number_of - 1), [1] * (number_of - 1)
    while spare > 0:
        free = [i for i in range(number_of - 1) if given[i] < reach]
        pool, left = sum([loads[i] for i in free]), spare
        for i in free:
            extra = min(reach - given[i], max(1, left * loads[i] // pool), spare)
            given[i] = given[i] + extra
            spare = spare - extra
    return np.array([reach] + given)


def ragged(own_key, amount, total, reach, skew):
    if amount == 2:
        one = jax.random.randint(own_key, (), max(1, total - reach), min(reach, total - 1) + 1)
        return jnp.stack([one, total - one])
    sizes = jnp.asarray(profile(amount, total, reach, skew), jnp.int32)
    twos = (amount - 1) // 2
    donor, receiver = sizes[1:1 + 2 * twos:2], sizes[2:2 + 2 * twos:2]
    slack = jnp.minimum(donor - 1, reach - receiver)
    shifted = jax.random.randint(jax.random.fold_in(own_key, 1), (twos,), 0, 1 << 20) % (slack + 1)
    sizes = sizes.at[1:1 + 2 * twos:2].set(donor - shifted).at[2:2 + 2 * twos:2].set(receiver + shifted)
    return sizes[jax.random.permutation(jax.random.fold_in(own_key, 2), amount)]


def scatter_about(stream_key, extent, scale, limit, pieces=(), kind=jnp.bfloat16):
    loudness = block_scale(stream_key, extent, pieces, -0.22, 0.18) if pieces else 1.0
    result = jax.random.normal(stream_key, extent, jnp.float32) * scale * loudness
    return jnp.minimum(jnp.maximum(result, -limit), limit).astype(kind)


def setup_inputs(seed: int = 0) -> dict:
    key_list = jax.random.split(jax.random.key(seed), 14)
    return {
        "hidden": scatter_about(key_list[0], (TOKENS, D), 1.0, 6.0, ((0, 16),)),
        "segment_ids": jax.vmap(lambda own: jnp.searchsorted(jnp.cumsum(ragged(own, DOCS_DEV, TOK_DEV, DOC_MOST, 2)), jnp.arange(TOK_DEV), side="right"))(jax.random.split(key_list[1], N_DP)).reshape((N_DP, TOK_DEV)).astype(jnp.int32),
        "attn_gain": jnp.clip(1.0 + 0.15 * jax.random.normal(key_list[2], (D,), jnp.float32), 0.25, 1.75),
        "w_query": draw_w_query(jax.random.fold_in(key_list[13], 71), 0),
        "w_key": draw_w_key(jax.random.fold_in(key_list[13], 71), 0),
        "w_value": scatter_about(key_list[5], (D, KVH * HD), D ** -0.5, 0.09375, ((1, 8),)),
        "w_out": scatter_about(key_list[6], (D, D), D ** -0.5, 0.09375, ((0, 8),)),
        "final_gain": jnp.clip(1.0 + 0.15 * jax.random.normal(key_list[7], (D,), jnp.float32), 0.25, 1.75),
        "adapter": scatter_about(key_list[8], (D, E), D ** -0.5, 0.09375),
        "features": scatter_about(key_list[9], (B, E), 1.0, 6.0, ((0, 128),)),
        "ln_gain": jnp.clip(1.0 + 0.15 * jax.random.normal(key_list[10], (E,), jnp.float32), 0.25, 1.75),
        "ln_bias": scatter_about(key_list[11], (E,), 0.5, 3.0, (), jnp.float32),
        "pair_ids": jax.random.permutation(key_list[12], B).astype(jnp.int32),
    }


SCALE = 1.0 / 0.07
EPS = 1e-05

def rotate(values, place):
    half = values.shape[-1] // 2
    freq = 500000.0 ** (-jnp.arange(half, dtype=jnp.float32) * 2.0 / values.shape[-1])
    angle = place[:, None] * freq[None, :]
    cosine = jnp.cos(angle)[:, None, :]
    sine = jnp.sin(angle)[:, None, :]
    first = values[..., :half]
    second = values[..., half:]
    return jnp.concatenate([first * cosine - second * sine, second * cosine + first * sine], axis=-1)

def positions(seg):
    before = lax.optimization_barrier(jnp.sum((seg[None, :] < seg[:, None]).astype(jnp.int32), axis=1))
    return (jnp.arange(seg.shape[0], dtype=jnp.int32) - before.astype(jnp.int32)).astype(jnp.float32)

def embed_text(projected):
    return projected * lax.rsqrt(lax.optimization_barrier(jnp.sum(projected * projected, axis=1, keepdims=True)) + 1e-06)

def embed_image(values, gain, shift):
    center = values - lax.optimization_barrier(jnp.mean(values, axis=1, keepdims=True))
    spread = lax.optimization_barrier(jnp.mean(center * center, axis=1, keepdims=True))
    normal = center * lax.rsqrt(spread + EPS) * gain + shift
    return normal * lax.rsqrt(lax.optimization_barrier(jnp.sum(normal * normal, axis=1, keepdims=True)) + 1e-06)

def text_shard(stream_b, seg, attn_gain, w_query, w_key, w_value, w_out, final_gain):
    length = stream_b.shape[0]
    stream = stream_b.astype(jnp.float32)
    normed = (stream * lax.rsqrt(lax.optimization_barrier(jnp.mean(stream * stream, axis=1, keepdims=True)) + EPS) * attn_gain).astype(jnp.bfloat16)
    place = positions(seg)
    query = rotate(jnp.dot(normed, w_query, preferred_element_type=jnp.float32).reshape(length, H, HD), place).astype(jnp.bfloat16)
    keys = rotate(jnp.dot(normed, w_key, preferred_element_type=jnp.float32).reshape(length, KVH, HD), place).astype(jnp.bfloat16)
    values = jnp.dot(normed, w_value, preferred_element_type=jnp.float32).astype(jnp.bfloat16).reshape(length, KVH, HD)
    query, keys, values = lax.optimization_barrier((query, keys, values))
    query_f = query.astype(jnp.float32).reshape(length, KVH, H // KVH, HD)
    score = jnp.einsum('tkgd,skd->kgts', query_f, keys.astype(jnp.float32)) * HD ** (-0.5)
    index = jnp.arange(length, dtype=jnp.int32)
    live = (seg[:, None] == seg[None, :]) & (index[:, None] >= index[None, :])
    top = lax.optimization_barrier(jnp.max(jnp.where(live, score, -jnp.inf), axis=-1, keepdims=True))
    weight = jnp.where(live, jnp.exp(score - top), 0.0)
    probs = (weight / lax.optimization_barrier(jnp.sum(weight, axis=-1, keepdims=True))).astype(jnp.bfloat16)
    probs = lax.optimization_barrier(probs)
    attended = jnp.einsum('kgts,skd->tkgd', probs.astype(jnp.float32), values.astype(jnp.float32))
    attended = lax.optimization_barrier(attended.astype(jnp.bfloat16).reshape(length, D))
    share = D // N_MP
    mixed = jnp.zeros((length, D), jnp.float32)
    for group in range(N_MP):
        term = jnp.dot(attended[:, group * share:(group + 1) * share], w_out[group * share:(group + 1) * share], preferred_element_type=jnp.float32).astype(jnp.bfloat16)
        term = lax.optimization_barrier(term)
        mixed = mixed + term.astype(jnp.float32)
    residual = stream + mixed
    final = residual * lax.rsqrt(lax.optimization_barrier(jnp.mean(residual * residual, axis=1, keepdims=True)) + EPS) * final_gain
    member = (jnp.arange(DOCS_DEV, dtype=jnp.int32)[:, None] == seg[None, :]).astype(jnp.float32)
    sums = jnp.dot(member, final, precision=lax.Precision.HIGHEST, preferred_element_type=jnp.float32)
    counts = lax.optimization_barrier(jnp.sum(member, axis=1))
    return (sums / counts[:, None]).astype(jnp.bfloat16)

def reference(hidden, segment_ids, attn_gain, w_query, w_key, w_value, w_out, final_gain, adapter, features, ln_gain, ln_bias, pair_ids):

    def one_sequence(items):
        return text_shard(items[0], items[1], attn_gain, w_query, w_key, w_value, w_out, final_gain)
    pooled = lax.map(one_sequence, (hidden.reshape(N_DP, TOK_DEV, D), segment_ids)).reshape(B, D)
    projected = jnp.dot(pooled, adapter, preferred_element_type=jnp.float32)
    image_input = features.astype(jnp.float32)
    match = (pair_ids[:, None] == jnp.arange(B, dtype=jnp.int32)[None, :]).astype(jnp.float32)

    def total_loss(projected_in, image_in):
        text_emb = embed_text(projected_in)
        image_emb = embed_image(image_in, ln_gain, ln_bias)
        scores = SCALE * jnp.dot(image_emb, text_emb.T, precision=lax.Precision.HIGHEST)
        image_lse = jnp.log(lax.optimization_barrier(jnp.sum(jnp.exp(scores), axis=1)))
        text_lse = jnp.log(lax.optimization_barrier(jnp.sum(jnp.exp(scores), axis=0)))
        positive = lax.optimization_barrier(jnp.sum(scores * match, axis=1))
        return (jnp.sum(image_lse) + jnp.sum(text_lse) - 2.0 * jnp.sum(positive)) / 2.0
    total, back = jax.vjp(total_loss, projected, image_input)
    grad_projected, feature_grad = back(jnp.ones_like(total))
    adapter_grad = jnp.dot(pooled.astype(jnp.float32).T, grad_projected, precision=lax.Precision.HIGHEST)
    return (total / B, adapter_grad, feature_grad)
```

```python
import jax
import jax.numpy as jnp
from jax import lax
from jax.sharding import PartitionSpec as P

HD = 128
DOCS_DEV = 16


SCALE = 1.0 / 0.07
EPS = 1e-05


def rotate(values, place):
    half = values.shape[-1] // 2
    freq = 500000.0 ** (-jnp.arange(half, dtype=jnp.float32) * 2.0 / values.shape[-1])
    angle = place[:, None] * freq[None, :]
    cosine = jnp.cos(angle)[:, None, :]
    sine = jnp.sin(angle)[:, None, :]
    first = values[..., :half]
    second = values[..., half:]
    return jnp.concatenate(
        [first * cosine - second * sine, second * cosine + first * sine], axis=-1
    )


def positions(seg):
    before = jnp.sum((seg[None, :] < seg[:, None]).astype(jnp.int32), axis=1)
    return (jnp.arange(seg.shape[0], dtype=jnp.int32) - before).astype(jnp.float32)


def embed_image(values, gain, shift):
    center = values - jnp.mean(values, axis=1, keepdims=True)
    spread = jnp.mean(center * center, axis=1, keepdims=True)
    normal = center * lax.rsqrt(spread + EPS) * gain + shift
    return normal * lax.rsqrt(jnp.sum(normal * normal, axis=1, keepdims=True) + 1e-06)


def on_device(
    hidden,
    segment_ids,
    attn_gain,
    w_query,
    w_key,
    w_value,
    w_out,
    final_gain,
    adapter,
    features,
    ln_gain,
    ln_bias,
    pair_ids,
):
    length = hidden.shape[0]
    width = hidden.shape[1]
    kv_local = w_key.shape[1] // HD
    q_local = w_query.shape[1] // HD
    group = q_local // kv_local
    tensor_count = lax.axis_size("mp")
    rows_dev = length // tensor_count
    mine = lax.axis_index("mp")
    every = lax.axis_index(("dp", "mp"))
    emb_rows = features.shape[0]
    seg = segment_ids[0]
    stream = hidden.astype(jnp.float32)
    normed = (
        stream * lax.rsqrt(jnp.mean(stream * stream, axis=1, keepdims=True) + EPS) * attn_gain
    ).astype(jnp.bfloat16)
    place = positions(seg)
    query = jnp.dot(normed, w_query, preferred_element_type=jnp.float32).reshape(
        length, q_local, HD
    )
    query = rotate(query, place).astype(jnp.bfloat16).reshape(length, kv_local, group, HD)
    keys = rotate(
        jnp.dot(normed, w_key, preferred_element_type=jnp.float32).reshape(length, kv_local, HD),
        place,
    ).astype(jnp.bfloat16)
    values = (
        jnp.dot(normed, w_value, preferred_element_type=jnp.float32)
        .astype(jnp.bfloat16)
        .reshape(length, kv_local, HD)
    )
    token_index = jnp.arange(length, dtype=jnp.int32)
    score = jnp.einsum("tkgd,skd->kgts", query, keys, preferred_element_type=jnp.float32) * HD ** (
        -0.5
    )
    live = (seg[:, None] == seg[None, :]) & (token_index[:, None] >= token_index[None, :])
    top = jnp.max(jnp.where(live, score, -jnp.inf), axis=-1, keepdims=True)
    weight = jnp.where(live, jnp.exp(score - top), 0.0)
    probs = (weight / jnp.sum(weight, axis=-1, keepdims=True)).astype(jnp.bfloat16)
    mixed_rows = jnp.einsum("kgts,skd->tkgd", probs, values, preferred_element_type=jnp.float32)
    pieces = mixed_rows.astype(jnp.bfloat16).reshape(length, q_local * HD)
    term = jnp.dot(pieces, w_out, preferred_element_type=jnp.float32).astype(jnp.bfloat16)
    terms = lax.all_to_all(
        term.reshape(tensor_count, rows_dev, width), "mp", 0, 0, tiled=True
    ).astype(jnp.float32)
    mixed = jnp.sum(terms, axis=0)
    residual = lax.dynamic_slice_in_dim(hidden, mine * rows_dev, rows_dev, 0) + mixed
    final = (
        residual
        * lax.rsqrt(jnp.mean(residual * residual, axis=1, keepdims=True) + EPS)
        * final_gain
    )
    doc_index = jnp.arange(DOCS_DEV, dtype=jnp.int32)
    seg_rows = lax.dynamic_slice_in_dim(seg, mine * rows_dev, rows_dev, 0)
    counts = jnp.sum((doc_index[:, None] == seg[None, :]).astype(jnp.float32), axis=1)
    member = (doc_index[:, None] == seg_rows[None, :]).astype(jnp.float32) / counts[:, None]
    doc_part = jnp.dot(
        member, final, precision=lax.Precision.HIGHEST, preferred_element_type=jnp.float32
    ).astype(jnp.bfloat16)
    proj_part = jnp.dot(doc_part, adapter, preferred_element_type=jnp.float32).astype(jnp.bfloat16)
    seqs = lax.axis_size("dp")
    own = width // (seqs * tensor_count)
    emb = adapter.shape[1]
    columns_by_peer = (
        doc_part.reshape(DOCS_DEV, seqs, tensor_count, own)
        .transpose(2, 0, 1, 3)
        .reshape(tensor_count, DOCS_DEV, seqs * own)
    )
    first = jnp.concatenate(
        [
            jnp.broadcast_to(proj_part[None], (tensor_count, DOCS_DEV, emb)),
            columns_by_peer,
            jnp.broadcast_to(
                features.reshape(1, DOCS_DEV, -1),
                (tensor_count, DOCS_DEV, emb_rows * emb // DOCS_DEV),
            ),
        ],
        axis=2,
    )
    first = lax.all_to_all(first, "mp", 0, 0, tiled=True)
    cut = emb + seqs * own
    sums = jnp.sum(first[:, :, :cut].astype(jnp.float32), axis=0).astype(jnp.bfloat16)
    feature_rows = first[:, :, cut:].reshape(tensor_count * emb_rows, emb)
    second = jnp.concatenate(
        [
            jnp.broadcast_to(sums[None, :, :emb], (seqs, DOCS_DEV, emb)),
            jnp.broadcast_to(feature_rows[None], (seqs, DOCS_DEV, emb)),
            sums[:, emb:].reshape(DOCS_DEV, seqs, own).transpose(1, 0, 2),
        ],
        axis=2,
    )
    second = lax.all_to_all(second, "dp", 0, 0, tiled=True)
    pair_count = seqs * DOCS_DEV
    second = second.reshape(pair_count, 2 * emb + own)
    projected = second[:, :emb].astype(jnp.float32)
    image_input = second[:, emb : 2 * emb].astype(jnp.float32)
    pooled_own = second[:, 2 * emb :].astype(jnp.float32)
    text_scale = lax.rsqrt(jnp.sum(projected * projected, axis=1, keepdims=True) + 1e-06)
    text_emb = projected * text_scale
    image_emb = embed_image(image_input, ln_gain, ln_bias)
    high = lax.Precision.HIGHEST
    columns = jnp.arange(pair_count, dtype=jnp.int32)
    match = (pair_ids[:, None] == columns[None, :]).astype(jnp.float32)
    scores = SCALE * jnp.dot(image_emb, text_emb.T, precision=high)
    image_lse = jnp.log(jnp.sum(jnp.exp(scores), axis=1, keepdims=True))
    text_lse = jnp.log(jnp.sum(jnp.exp(scores), axis=0, keepdims=True))
    loss = (jnp.sum(image_lse) + jnp.sum(text_lse) - 2.0 * jnp.sum(scores * match)) / (
        2.0 * pair_count
    )
    dual = 0.5 * (jnp.exp(scores - image_lse) + jnp.exp(scores - text_lse)) - match
    grad_text = SCALE * jnp.dot(dual.T, image_emb, precision=high)
    grad_projected = text_scale * (
        grad_text - text_emb * jnp.sum(grad_text * text_emb, axis=1, keepdims=True)
    )
    adapter_grad = jnp.dot(pooled_own.T, grad_projected, precision=high)
    dual_own = lax.dynamic_slice_in_dim(dual, every * emb_rows, emb_rows, 0)
    grad_image_emb = SCALE * jnp.dot(dual_own, text_emb, precision=high)
    _, back_image = jax.vjp(
        lambda values_in: embed_image(values_in, ln_gain, ln_bias), features.astype(jnp.float32)
    )
    feature_grad = back_image(grad_image_emb)[0]
    return (loss, adapter_grad, feature_grad)


def solution(mesh):
    return jax.shard_map(
        on_device,
        mesh=mesh,
        in_specs=(
            P("dp", None),
            P("dp", None),
            P(),
            P(None, "mp"),
            P(None, "mp"),
            P(None, "mp"),
            P("mp", None),
            P(),
            P(),
            P(("dp", "mp"), None),
            P(),
            P(),
            P(),
        ),
        out_specs=(P(), P(("dp", "mp"), None), P(("dp", "mp"), None)),
        check_vma=False,
    )
```

```python
import jax
import jax.numpy as jnp
import numpy as np
from jax import lax
from jax.experimental import pallas as pl
from jax.experimental.pallas import tpu as pltpu
from jax.sharding import PartitionSpec as P

HD = 128
DOCS_DEV = 16
SCALE = 1.0 / 0.07
EPS = 1e-05
HIGH = lax.Precision.HIGHEST
F32 = jnp.float32
BF16 = jnp.bfloat16


def rope_tables(length):
    half = HD // 2
    freq = 500000.0 ** (-np.arange(half) * 2.0 / HD)
    angle = np.arange(length)[:, None] * freq[None, :]
    cosine = np.concatenate([np.cos(angle), np.cos(angle)], axis=1)
    sine = np.concatenate([-np.sin(angle), np.sin(angle)], axis=1)
    return cosine.astype(np.float32), sine.astype(np.float32)


def dot(left, right, precision=None):
    return jnp.dot(left, right, precision=precision, preferred_element_type=F32)


def dot_rows(left, right, precision=None):
    return lax.dot_general(
        left, right, (((1,), (1,)), ((), ())), precision=precision, preferred_element_type=F32
    )


def text_kernel(
    place, hidden, w_query, w_key, w_value, w_out, gain, cosine, sine, seg,
    z_send, z_keep, block_0, block_1, block_2, block_3,
    hid, w_in, w_up, acc, query, keys, values, att, ordered, stage, stage_keep, stage_send, sems, out_sems,
):
    length, width = hidden.shape
    q_local = w_query.shape[1] // HD
    parts = 4
    span = width // parts
    q_cols = w_query.shape[1]
    kv_cols = w_key.shape[1]
    copies = []
    for part in range(parts):
        rows = pl.ds(part * span, span)
        group = [
            pltpu.make_async_copy(hidden.at[:, rows], hid.at[:, rows], sems.at[part, 0]),
            pltpu.make_async_copy(
                w_query.at[rows, :], w_in.at[rows, pl.ds(0, q_cols)], sems.at[part, 1]
            ),
            pltpu.make_async_copy(
                w_key.at[rows, :], w_in.at[rows, pl.ds(q_cols, kv_cols)], sems.at[part, 2]
            ),
            pltpu.make_async_copy(
                w_value.at[rows, :], w_in.at[rows, pl.ds(q_cols + kv_cols, kv_cols)], sems.at[part, 3]
            ),
        ]
        for copy in group:
            copy.start()
        copies.append(group)
    up_copy = pltpu.make_async_copy(w_out, w_up, sems.at[parts, 0])
    up_copy.start()
    squares = jnp.zeros((length, HD), F32)
    for part in range(parts):
        for copy in copies[part]:
            copy.wait()
        cols = slice(part * span, (part + 1) * span)
        stream = hid[:, cols].astype(F32)
        for lane in range(0, span, HD):
            piece = stream[:, lane : lane + HD]
            squares = squares + piece * piece
        scaled = (stream * gain[:, cols]).astype(BF16)
        product = dot(scaled, w_in[cols, :])
        if part == 0:
            acc[...] = product
        else:
            acc[...] += product
    norm = lax.rsqrt(jnp.sum(squares, axis=1, keepdims=True) * (1.0 / width) + EPS)
    cos_t = cosine[...] * norm
    sin_t = sine[...] * norm
    for head in range(q_local):
        lanes = slice(head * HD, (head + 1) * HD)
        value = acc[:, lanes]
        query[:, lanes] = (value * cos_t + pltpu.roll(value, HD // 2, 1) * sin_t).astype(BF16)
    value = acc[:, q_cols : q_cols + HD]
    keys[...] = (value * cos_t + pltpu.roll(value, HD // 2, 1) * sin_t).astype(BF16)
    values[...] = (acc[:, q_cols + HD :] * norm).astype(BF16)
    block = 128
    seg_f = seg[...].astype(F32)
    for at in range(length // block):
        first = max(0, at - 1) * block
        last = (at + 1) * block
        rows = slice(at * block, last)
        seg_q = jnp.broadcast_to(seg_f[:, rows], (block, block)).T
        masks = []
        for key_at in range(first, last, block):
            seg_k = jnp.broadcast_to(seg_f[:, key_at : key_at + block], (block, block))
            live = seg_q == seg_k
            if key_at == at * block:
                live = live & (
                    lax.broadcasted_iota(jnp.int32, (block, block), 0)
                    >= lax.broadcasted_iota(jnp.int32, (block, block), 1)
                )
            masks.append(jnp.where(live, 0.0, -1e30))
        mask = masks[0] if len(masks) == 1 else jnp.concatenate(masks, axis=1)
        mask = jnp.concatenate([mask] * q_local, axis=0)
        stacked = jnp.concatenate(
            [query[rows, head * HD : (head + 1) * HD] for head in range(q_local)], axis=0
        )
        score = dot_rows(stacked, keys[first:last, :]) * HD ** (-0.5) + mask
        weight = jnp.exp(score - jnp.max(score, axis=1, keepdims=True))
        probs = (weight / jnp.sum(weight, axis=1, keepdims=True)).astype(BF16)
        result = dot(probs, values[first:last, :]).astype(BF16)
        for head in range(q_local):
            att[rows, head * HD : (head + 1) * HD] = result[head * block : (head + 1) * block]
    y, z = place[0], place[1]
    small = length // 8
    for step in range(4):
        base = lax.rem(y + step, 4) * 2
        mine = pl.multiple_of((base + z) * small, small)
        other = pl.multiple_of((base + 1 - z) * small, small)
        at = 2 * step * small
        ordered[pl.ds(at, small), :] = att[pl.ds(mine, small), :]
        ordered[pl.ds(at + small, small), :] = att[pl.ds(other, small), :]
    up_copy.wait()
    chunk = 512
    cut = block_0.shape[1]
    sends = []

    def ship(source, target):
        send = pltpu.make_async_copy(source, target, out_sems.at[len(sends)])
        send.start()
        sends.append(send)

    for at in range(cut, width, chunk):
        result = dot(ordered[...], w_up[:, at : at + chunk]).astype(BF16)
        cols = slice(at - cut, at - cut + chunk)
        for step in range(4):
            row = 2 * step * small
            stage_keep[step * small : (step + 1) * small, cols] = result[row : row + small]
            stage_send[step * small : (step + 1) * small, cols] = result[
                row + small : row + 2 * small
            ]
    ship(stage_send, z_send)
    ship(stage_keep, z_keep)
    for at in range(0, cut, chunk):
        cols = slice(at, at + chunk)
        stage[:, cols] = dot(ordered[...], w_up[:, cols]).astype(BF16)
    for ref, step in ((block_2, 2), (block_1, 1), (block_3, 3), (block_0, 0)):
        ship(stage.at[pl.ds(2 * small * step, 2 * small), :], ref)
    for send in sends:
        send.wait()


def fetch_kernel(place, hidden, adapter, after, rows, weights, sems):
    small = rows.shape[0]
    start = pl.multiple_of((place[0] * 2 + place[1]) * small, small)
    copies = [
        pltpu.make_async_copy(hidden.at[pl.ds(start, small), :], rows, sems.at[0]),
        pltpu.make_async_copy(adapter, weights, sems.at[1]),
    ]
    for copy in copies:
        copy.start()
    for copy in copies:
        copy.wait()


def pool_kernel(
    rows, adapter, member, gain, features, a_own, a_1, a_2, a_3, a_z, b_own, b_1, b_2, b_3,
    message, doc,
):
    small, width = rows.shape
    cut = a_z.shape[1]
    left = a_own[0:small, :].astype(F32)
    for piece in (a_1, a_2, a_3):
        left = left + piece[0:small, :].astype(F32)
    left = left + a_z[...].astype(F32) + rows[:, 0:cut].astype(F32)
    right = b_own[...].astype(F32)
    for piece in (b_1, b_2, b_3):
        right = right + piece[...].astype(F32)
    right = right + rows[:, cut:].astype(F32)
    residual = jnp.concatenate([left, right], axis=1)
    norm = lax.rsqrt(jnp.sum(residual * residual, axis=1, keepdims=True) * (1.0 / width) + EPS)
    final = residual * norm * gain[...]
    means = dot(member[...], final, HIGH)
    doc[...] = means.astype(BF16)
    emb = adapter.shape[1]
    projected = dot(doc[...], adapter[...])
    projected = projected.astype(BF16)
    own = 32
    seqs = 16
    lane = lax.broadcasted_iota(jnp.int32, (DOCS_DEV, HD), 1) // own
    for peer in range(8):
        message[peer, :, 0:emb] = projected
        for group in range(seqs // 4):
            tile = None
            for slot in range(4):
                at = (2 * (group * 4 + slot) + peer // 4) * HD
                piece = means[:, at : at + HD]
                shift = ((slot - peer % 4) * own) % HD
                if shift:
                    piece = pltpu.roll(piece, shift, 1)
                tile = piece if tile is None else jnp.where(lane == slot, piece, tile)
            message[peer, :, emb + group * HD : emb + (group + 1) * HD] = tile.astype(BF16)
    image_rows = features[...].astype(F32)
    per_row = emb // HD
    lined = jnp.concatenate(
        [
            image_rows[row : row + 1, at * HD : (at + 1) * HD]
            for row in range(features.shape[0])
            for at in range(per_row)
        ],
        axis=0,
    ).astype(BF16)
    for peer in range(8):
        message[peer, :, emb + seqs * own :] = lined


def sum_kernel(message, second, images):
    emb = images.shape[1]
    cut = message.shape[2] - HD
    total = message[0, :, 0:cut].astype(F32)
    for peer in range(1, message.shape[0]):
        total = total + message[peer, :, 0:cut].astype(F32)
    total = total.astype(BF16)
    per_row = emb // HD
    for peer in range(message.shape[0]):
        lined = message[peer, :, cut:].astype(F32)
        for at in range(lined.shape[0]):
            row = peer * (lined.shape[0] // per_row) + at // per_row
            lane = (at % per_row) * HD
            images[row : row + 1, lane : lane + HD] = lined[at : at + 1, :]
    image_rows = images[...].astype(BF16)
    for seq in range(second.shape[0]):
        second[seq, :, 0:emb] = total[:, 0:emb]
        at = emb + (seq // 4) * HD
        second[seq, :, emb : emb + HD] = total[:, at : at + HD]
        second[seq, :, emb + HD :] = image_rows


def image_tower(values, gain, shift):
    center = values - jnp.mean(values, axis=1, keepdims=True)
    spread = lax.rsqrt(jnp.mean(center * center, axis=1, keepdims=True) + EPS)
    unit = center * spread
    normal = unit * gain + shift
    scale = lax.rsqrt(jnp.sum(normal * normal, axis=1, keepdims=True) + 1e-06)
    return unit, spread, normal * scale, scale


def loss_kernel(
    place, gathered, features, ln_gain, ln_bias, pairs, loss, adapter_grad, feature_grad, wide
):
    count = gathered.shape[0]
    emb = features.shape[1]
    projected = gathered[:, 0:emb].astype(F32)
    text_scale = lax.rsqrt(jnp.sum(projected * projected, axis=1, keepdims=True) + 1e-06)
    text = projected * text_scale
    image = image_tower(gathered[:, emb + HD :].astype(F32), ln_gain[...], ln_bias[...])[2]
    scores = SCALE * dot_rows(image, text, HIGH)
    grown = jnp.exp(scores)
    row_sum = jnp.sum(grown, axis=1, keepdims=True)
    col_sum = jnp.sum(grown, axis=0, keepdims=True)
    columns = lax.broadcasted_iota(jnp.int32, (count, count), 1)
    match = (pairs[...] == columns).astype(F32)
    loss[...] = (
        jnp.sum(jnp.log(row_sum), axis=0, keepdims=True)
        + jnp.sum(jnp.log(col_sum), axis=1, keepdims=True)
        - 2.0 * jnp.sum(jnp.sum(scores * match, axis=1, keepdims=True), axis=0, keepdims=True)
    ) * (1.0 / (2.0 * count))
    dual = 0.5 * grown * (1.0 / row_sum + 1.0 / col_sum) - match
    grad_text = SCALE * dot(dual.T, image, HIGH)
    grad_projected = text_scale * (
        grad_text - text * jnp.sum(grad_text * text, axis=1, keepdims=True)
    )
    pooled = gathered[:, emb : emb + HD].astype(F32)
    wide[...] = dot(pooled.T, grad_projected, HIGH)
    own = adapter_grad.shape[0]
    slot = pl.multiple_of(place[2] * own, own)
    adapter_grad[...] = wide[pl.ds(slot, own), :]
    few = features.shape[0]
    chosen = (
        lax.broadcasted_iota(jnp.int32, (few, count), 1)
        == place[3] + lax.broadcasted_iota(jnp.int32, (few, count), 0)
    ).astype(F32)
    dual_own = dot(chosen, dual, HIGH)
    grad_image = SCALE * dot(dual_own, text, HIGH)
    unit, spread, mine, scale = image_tower(
        features[...].astype(F32), ln_gain[...], ln_bias[...]
    )
    grad_normal = scale * (grad_image - mine * jnp.sum(grad_image * mine, axis=1, keepdims=True))
    grad_unit = grad_normal * ln_gain[...]
    feature_grad[...] = spread * (
        grad_unit
        - jnp.mean(grad_unit, axis=1, keepdims=True)
        - unit * jnp.mean(grad_unit * unit, axis=1, keepdims=True)
    )


def y_shift(step):
    return [(y * 2 + z, ((y + step) % 4) * 2 + z) for y in range(4) for z in range(2)]


Z_SWAP = [(m, m ^ 1) for m in range(8)]


def on_device(
    hidden,
    segment_ids,
    attn_gain,
    w_query,
    w_key,
    w_value,
    w_out,
    final_gain,
    adapter,
    features,
    ln_gain,
    ln_bias,
    pair_ids,
):
    length, width = hidden.shape
    emb_rows, emb = features.shape
    tensor_count = lax.axis_size("mp")
    seqs = lax.axis_size("dp")
    mine = lax.axis_index("mp")
    seq = lax.axis_index("dp")
    every = lax.axis_index(("dp", "mp"))
    place = jnp.stack([mine // 2, mine % 2, seq % 4, every * emb_rows]).astype(jnp.int32)
    params = pltpu.CompilerParams(vmem_limit_bytes=16 * 1024 * 1024)
    whole = pl.BlockSpec(memory_space=pltpu.VMEM)
    scalar = pl.BlockSpec(memory_space=pltpu.SMEM)
    anywhere = pl.BlockSpec(memory_space=pl.ANY)
    small = length // 8
    cut = 2560
    q_cols = w_query.shape[1]
    kv_cols = w_key.shape[1]
    cosine, sine = rope_tables(length)
    late = jax.ShapeDtypeStruct((4 * small, width - cut), BF16)
    early = jax.ShapeDtypeStruct((2 * small, cut), BF16)
    send, keep, a_own, a_1, a_2, a_3 = pl.pallas_call(
        text_kernel,
        out_shape=[late] * 2 + [early] * 4,
        in_specs=[scalar] + [anywhere] * 5 + [whole] * 4,
        out_specs=[anywhere] * 6,
        scratch_shapes=[
            pltpu.VMEM((length, width), BF16),
            pltpu.VMEM((width, q_cols + 2 * kv_cols), BF16),
            pltpu.VMEM((q_cols, width), BF16),
            pltpu.VMEM((length, q_cols + 2 * kv_cols), F32),
            pltpu.VMEM((length, q_cols), BF16),
            pltpu.VMEM((length, kv_cols), BF16),
            pltpu.VMEM((length, kv_cols), BF16),
            pltpu.VMEM((length, q_cols), BF16),
            pltpu.VMEM((length, q_cols), BF16),
            pltpu.VMEM((length, cut), BF16),
            pltpu.VMEM(late.shape, BF16),
            pltpu.VMEM(late.shape, BF16),
            pltpu.SemaphoreType.DMA((5, 4)),
            pltpu.SemaphoreType.DMA((6,)),
        ],
        compiler_params=pltpu.CompilerParams(vmem_limit_bytes=56 * 1024 * 1024),
        name="text_tower",
    )(
        place, hidden, w_query, w_key, w_value, w_out, attn_gain.reshape(1, width),
        jnp.asarray(cosine), jnp.asarray(sine), segment_ids,
    )
    swapped = lax.ppermute(send, "mp", Z_SWAP)
    r_2 = lax.ppermute(a_2, "mp", y_shift(2))
    r_1 = lax.ppermute(a_1, "mp", y_shift(1))
    r_3 = lax.ppermute(a_3, "mp", y_shift(3))
    rows, weights = pl.pallas_call(
        fetch_kernel,
        out_shape=[
            jax.ShapeDtypeStruct((small, width), BF16),
            jax.ShapeDtypeStruct(adapter.shape, BF16),
        ],
        in_specs=[scalar] + [anywhere] * 3,
        out_specs=[whole] * 2,
        scratch_shapes=[pltpu.SemaphoreType.DMA((2,))],
        compiler_params=params,
        name="fetch_weights",
    )(place, hidden, adapter, a_own)
    halves = (keep.astype(F32) + swapped.astype(F32)).astype(BF16)
    b_own, b_1, b_2, b_3 = [halves[k * small : (k + 1) * small] for k in range(4)]
    q_2 = lax.ppermute(b_2, "mp", y_shift(2))
    q_1 = lax.ppermute(b_1, "mp", y_shift(1))
    q_3 = lax.ppermute(b_3, "mp", y_shift(3))
    a_send = (
        a_own[small:].astype(F32)
        + r_1[small:].astype(F32)
        + r_2[small:].astype(F32)
        + r_3[small:].astype(F32)
    ).astype(BF16)
    a_z = lax.ppermute(a_send, "mp", Z_SWAP)
    seg = segment_ids[0]
    docs = jnp.arange(DOCS_DEV, dtype=jnp.int32)[:, None]
    counts = jnp.sum((docs == seg[None, :]).astype(F32), axis=1, keepdims=True)
    seg_rows = lax.dynamic_slice_in_dim(seg, mine * small, small, 0)
    member = (docs == seg_rows[None, :]).astype(F32) / counts
    own_cols = width // tensor_count
    message = pl.pallas_call(
        pool_kernel,
        out_shape=jax.ShapeDtypeStruct((tensor_count, DOCS_DEV, emb + own_cols + HD), BF16),
        in_specs=[whole] * 14,
        out_specs=whole,
        scratch_shapes=[pltpu.VMEM((DOCS_DEV, width), BF16)],
        compiler_params=params,
        name="pool_and_project",
    )(
        rows, weights, member, final_gain.reshape(1, width), features,
        a_own, r_1, r_2, r_3, a_z, b_own, q_1, q_2, q_3,
    )
    message = lax.all_to_all(message, "mp", 0, 0, tiled=True)
    second = pl.pallas_call(
        sum_kernel,
        out_shape=jax.ShapeDtypeStruct((seqs, DOCS_DEV, 2 * emb + HD), BF16),
        in_specs=[whole],
        out_specs=whole,
        scratch_shapes=[pltpu.VMEM((DOCS_DEV, emb), F32)],
        compiler_params=params,
        name="sum_partials",
    )(message)
    second = lax.all_to_all(second, "dp", 0, 0, tiled=True)
    count = seqs * DOCS_DEV
    own = width // (seqs * tensor_count)
    loss, adapter_grad, feature_grad = pl.pallas_call(
        loss_kernel,
        out_shape=[
            jax.ShapeDtypeStruct((1, 1), F32),
            jax.ShapeDtypeStruct((own, emb), F32),
            jax.ShapeDtypeStruct((emb_rows, emb), F32),
        ],
        in_specs=[scalar] + [whole] * 5,
        out_specs=[whole] * 3,
        scratch_shapes=[pltpu.VMEM((HD, emb), F32)],
        compiler_params=params,
        name="loss_and_gradients",
    )(
        place, second.reshape(count, 2 * emb + HD), features,
        ln_gain.reshape(1, emb), ln_bias.reshape(1, emb), pair_ids.reshape(count, 1),
    )
    return (loss[0, 0], adapter_grad, feature_grad)


def solution(mesh):
    return jax.shard_map(
        on_device,
        mesh=mesh,
        in_specs=(
            P("dp", None),
            P("dp", None),
            P(),
            P(None, "mp"),
            P(None, "mp"),
            P(None, "mp"),
            P("mp", None),
            P(),
            P(),
            P(("dp", "mp"), None),
            P(),
            P(),
            P(),
        ),
        out_specs=(P(), P(("dp", "mp"), None), P(("dp", "mp"), None)),
        check_vma=False,
    )
```

```python
import jax
import jax.numpy as jnp
import numpy as np
from jax import lax
from jax.experimental import pallas as pl
from jax.experimental.pallas import tpu as pltpu
from jax.sharding import PartitionSpec as P

HD = 128
DOCS_DEV = 16
SCALE = 1.0 / 0.07
EPS = 1e-05
HIGH = lax.Precision.HIGHEST
F32 = jnp.float32
BF16 = jnp.bfloat16


def rope_tables(length):
    half = HD // 2
    freq = 500000.0 ** (-np.arange(half) * 2.0 / HD)
    angle = np.arange(length)[:, None] * freq[None, :]
    cosine = np.concatenate([np.cos(angle), np.cos(angle)], axis=1)
    sine = np.concatenate([-np.sin(angle), np.sin(angle)], axis=1)
    return cosine.astype(np.float32), sine.astype(np.float32)


def dot(left, right, precision=None):
    return jnp.dot(left, right, precision=precision, preferred_element_type=F32)


def dot_rows(left, right, precision=None):
    return lax.dot_general(
        left, right, (((1,), (1,)), ((), ())), precision=precision, preferred_element_type=F32
    )


def text_kernel(
    hidden, w_query, w_key, w_value, w_out, gain, cosine, sine, seg,
    z_send, z_keep, up_1, down_1, up_2, down_2, block_0,
    hid, w_in, w_up, table, acc, query, keys, values, att, ordered, stage, stage_keep, stage_send, sems, out_sems,
):
    length, width = hidden.shape
    q_local = w_query.shape[1] // HD
    parts = 4
    span = width // parts
    q_cols = w_query.shape[1]
    kv_cols = w_key.shape[1]
    copies = []
    for part in range(parts):
        rows = pl.ds(part * span, span)
        group = [
            pltpu.make_async_copy(hidden.at[:, rows], hid.at[:, rows], sems.at[part, 0]),
            pltpu.make_async_copy(
                w_query.at[rows, :], w_in.at[rows, pl.ds(0, q_cols)], sems.at[part, 1]
            ),
            pltpu.make_async_copy(
                w_key.at[rows, :], w_in.at[rows, pl.ds(q_cols, kv_cols)], sems.at[part, 2]
            ),
            pltpu.make_async_copy(
                w_value.at[rows, :], w_in.at[rows, pl.ds(q_cols + kv_cols, kv_cols)], sems.at[part, 3]
            ),
        ]
        for copy in group:
            copy.start()
        copies.append(group)
    table_copies = [
        pltpu.make_async_copy(cosine, table.at[0], sems.at[parts, 1]),
        pltpu.make_async_copy(sine, table.at[1], sems.at[parts, 2]),
    ]
    for copy in table_copies:
        copy.start()
    up_copy = pltpu.make_async_copy(w_out, w_up, sems.at[parts, 0])
    up_copy.start()
    squares = jnp.zeros((length, HD), F32)
    for part in range(parts):
        for copy in copies[part]:
            copy.wait()
        cols = slice(part * span, (part + 1) * span)
        stream = hid[:, cols].astype(F32)
        for lane in range(0, span, HD):
            piece = stream[:, lane : lane + HD]
            squares = squares + piece * piece
        scaled = (stream * gain[:, cols]).astype(BF16)
        product = dot(scaled, w_in[cols, :])
        if part == 0:
            acc[...] = product
        else:
            acc[...] += product
    norm = lax.rsqrt(jnp.sum(squares, axis=1, keepdims=True) * (1.0 / width) + EPS)
    for copy in table_copies:
        copy.wait()
    cos_t = table[0] * norm
    sin_t = table[1] * norm
    value = acc[:, q_cols : q_cols + HD]
    keys[...] = (value * cos_t + pltpu.roll(value, HD // 2, 1) * sin_t).astype(BF16)
    values[:, 0:HD] = (acc[:, q_cols + HD :] * norm).astype(BF16)
    values[:, HD:] = jnp.ones((length, HD), BF16)
    cos_t = cos_t * HD ** (-0.5)
    sin_t = sin_t * HD ** (-0.5)
    for head in range(q_local):
        lanes = slice(head * HD, (head + 1) * HD)
        value = acc[:, lanes]
        query[:, lanes] = (value * cos_t + pltpu.roll(value, HD // 2, 1) * sin_t).astype(BF16)
    block = 128
    seg_f = seg[...].astype(F32)
    for at in range(length // block):
        first = max(0, at - 1) * block
        last = (at + 1) * block
        rows = slice(at * block, last)
        seg_q = jnp.broadcast_to(seg_f[:, rows], (block, block)).T
        masks = []
        for key_at in range(first, last, block):
            seg_k = jnp.broadcast_to(seg_f[:, key_at : key_at + block], (block, block))
            live = seg_q == seg_k
            if key_at == at * block:
                live = live & (
                    lax.broadcasted_iota(jnp.int32, (block, block), 0)
                    >= lax.broadcasted_iota(jnp.int32, (block, block), 1)
                )
            masks.append(jnp.where(live, 0.0, -1e30))
        mask = masks[0] if len(masks) == 1 else jnp.concatenate(masks, axis=1)
        mask = jnp.concatenate([mask] * q_local, axis=0)
        stacked = jnp.concatenate(
            [query[rows, head * HD : (head + 1) * HD] for head in range(q_local)], axis=0
        )
        score = dot_rows(stacked, keys[first:last, :]) + mask
        weight = jnp.exp(score - jnp.max(score, axis=1, keepdims=True)).astype(BF16)
        result = dot(weight, values[first:last, :])
        result = (result[:, 0:HD] / result[:, HD:]).astype(BF16)
        for head in range(q_local):
            att[rows, head * HD : (head + 1) * HD] = result[head * block : (head + 1) * block]
    index = lax.axis_index("mp")
    y, z = index // 2, lax.rem(index, 2)
    small = length // 8
    for step in range(4):
        base = lax.rem(y + step, 4) * 2
        mine = pl.multiple_of((base + z) * small, small)
        other = pl.multiple_of((base + 1 - z) * small, small)
        at = 2 * step * small
        ordered[pl.ds(at, small), :] = att[pl.ds(mine, small), :]
        ordered[pl.ds(at + small, small), :] = att[pl.ds(other, small), :]
    up_copy.wait()
    chunk = 512
    cut = block_0.shape[1]
    side = cut // 2
    sends = []

    def ship(source, target):
        send = pltpu.make_async_copy(source, target, out_sems.at[len(sends)])
        send.start()
        sends.append(send)

    def block(step, lane):
        return stage.at[pl.ds(2 * small * step, 2 * small), pl.ds(lane, side)]

    for at in range(0, cut, chunk):
        cols = slice(at, min(at + chunk, cut))
        stage[:, cols] = dot(ordered[...], w_up[:, cols]).astype(BF16)
    ship(block(2, 0), up_1.at[pl.ds(0, 2 * small), :])
    ship(block(1, side), up_1.at[pl.ds(2 * small, 2 * small), :])
    ship(block(2, side), down_1.at[pl.ds(0, 2 * small), :])
    ship(block(3, 0), down_1.at[pl.ds(2 * small, 2 * small), :])
    ship(block(1, 0), up_2)
    ship(block(3, side), down_2)
    ship(stage.at[pl.ds(0, 2 * small), :], block_0)
    for at in range(cut, width, chunk):
        result = dot(ordered[...], w_up[:, at : min(at + chunk, width)]).astype(BF16)
        cols = slice(at - cut, min(at + chunk, width) - cut)
        for step in range(4):
            row = 2 * step * small
            stage_keep[step * small : (step + 1) * small, cols] = result[row : row + small]
            stage_send[step * small : (step + 1) * small, cols] = result[
                row + small : row + 2 * small
            ]
        piece = pl.ds(at - cut, min(at + chunk, width) - at)
        ship(stage_send.at[:, piece], z_send.at[:, piece])
        ship(stage_keep.at[:, piece], z_keep.at[:, piece])
    for send in sends:
        send.wait()


def add(left, right):
    return (left.astype(F32) + right.astype(F32)).astype(BF16)


def pass_on_kernel(up_2, down_2, up_1, down_1, up, down, got, sems):
    rows = up.shape[0]
    copies = [
        pltpu.make_async_copy(source.at[pl.ds(0, rows), :], got.at[at], sems.at[at])
        for at, source in enumerate((up_2, up_1, down_2, down_1))
    ]
    for copy in copies:
        copy.start()
    for at, target in enumerate((up, down)):
        copies[2 * at].wait()
        copies[2 * at + 1].wait()
        target[...] = add(got[2 * at], got[2 * at + 1])


def swap_kernel(keep, swapped, after, block_0, block_1, block_2, block_3):
    size = block_0.shape[0]
    for step, block in enumerate((block_0, block_1, block_2, block_3)):
        rows = slice(step * size, (step + 1) * size)
        block[...] = add(keep[rows, :], swapped[rows, :])


def fold_kernel(own, up_1, down_1, up_2, down_2, after, kept, sent):
    small = kept.shape[0]
    total = ring_sum(own, up_1, down_1, up_2, down_2)
    kept[...] = total[:small]
    sent[...] = total[small:].astype(BF16)


def fetch_kernel(adapter, after, weights, sem):
    copy = pltpu.make_async_copy(adapter, weights, sem)
    copy.start()
    copy.wait()


def ring_sum(own, up_1, down_1, up_2, down_2):
    rows, width = own.shape
    side = width // 2
    left = own[:, 0:side].astype(F32) + down_1[rows:, :].astype(F32) + up_2[...].astype(F32)
    right = own[:, side:].astype(F32) + up_1[rows:, :].astype(F32) + down_2[...].astype(F32)
    return jnp.concatenate([left, right], axis=1)


def pool_kernel(
    rows, adapter, member, gain, features, kept, a_z, b_own, b_1, b_2, b_3, message, doc,
):
    small, width = rows.shape
    left = kept[...] + a_z[...].astype(F32)
    right = b_own[...].astype(F32) + b_1[...].astype(F32)
    right = right + b_2[...].astype(F32) + b_3[...].astype(F32)
    residual = jnp.concatenate([left, right], axis=1) + rows[...].astype(F32)
    norm = lax.rsqrt(jnp.sum(residual * residual, axis=1, keepdims=True) * (1.0 / width) + EPS)
    final = residual * norm * gain[...]
    means = dot(member[...], final, HIGH)
    doc[...] = means.astype(BF16)
    emb = adapter.shape[1]
    projected = dot(doc[...], adapter[...])
    projected = projected.astype(BF16)
    own = 32
    seqs = 16
    lane = lax.broadcasted_iota(jnp.int32, (DOCS_DEV, HD), 1) // own
    for peer in range(8):
        message[peer, :, 0:emb] = projected
        for group in range(seqs // 4):
            tile = None
            for slot in range(4):
                at = (2 * (group * 4 + slot) + peer // 4) * HD
                piece = means[:, at : at + HD]
                shift = ((slot - peer % 4) * own) % HD
                if shift:
                    piece = pltpu.roll(piece, shift, 1)
                tile = piece if tile is None else jnp.where(lane == slot, piece, tile)
            message[peer, :, emb + group * HD : emb + (group + 1) * HD] = tile.astype(BF16)
    image_rows = features[...].astype(F32)
    per_row = emb // HD
    lined = jnp.concatenate(
        [
            image_rows[row : row + 1, at * HD : (at + 1) * HD]
            for row in range(features.shape[0])
            for at in range(per_row)
        ],
        axis=0,
    ).astype(BF16)
    for peer in range(8):
        message[peer, :, emb + seqs * own :] = lined


def sum_kernel(message, second, images):
    emb = images.shape[1]
    cut = message.shape[2] - HD
    total = message[0, :, 0:cut].astype(F32)
    for peer in range(1, message.shape[0]):
        total = total + message[peer, :, 0:cut].astype(F32)
    total = total.astype(BF16)
    per_row = emb // HD
    for peer in range(message.shape[0]):
        lined = message[peer, :, cut:].astype(F32)
        for at in range(lined.shape[0]):
            row = peer * (lined.shape[0] // per_row) + at // per_row
            lane = (at % per_row) * HD
            images[row : row + 1, lane : lane + HD] = lined[at : at + 1, :]
    image_rows = images[...].astype(BF16)
    for chip in range(second.shape[0]):
        second[chip, :, 0:emb] = total[:, 0:emb]
        at = emb + (chip // 2) * HD
        second[chip, :, emb : emb + HD] = total[:, at : at + HD]
        second[chip, :, emb + HD :] = image_rows


def image_tower(values, gain, shift):
    center = values - jnp.mean(values, axis=1, keepdims=True)
    spread = lax.rsqrt(jnp.mean(center * center, axis=1, keepdims=True) + EPS)
    unit = center * spread
    normal = unit * gain + shift
    scale = lax.rsqrt(jnp.sum(normal * normal, axis=1, keepdims=True) + 1e-06)
    return unit, spread, normal * scale, scale


def split(value):
    high = value.astype(BF16)
    return high, (value - high.astype(F32)).astype(BF16)


def loss_kernel(
    same, other, features, ln_gain, ln_bias, pairs, loss, adapter_grad, feature_grad, all_rows, wide
):
    count = all_rows.shape[0]
    emb = features.shape[1]
    core = lax.rem(lax.axis_index("dp"), 2)
    for chip in range(count // (2 * DOCS_DEV)):
        rows = slice(chip * DOCS_DEV, (chip + 1) * DOCS_DEV)
        for ref, at in ((same, core), (other, 1 - core)):
            start = pl.multiple_of((2 * chip + at) * DOCS_DEV, DOCS_DEV)
            all_rows[pl.ds(start, DOCS_DEV), :] = ref[rows, :]
    image = image_tower(all_rows[:, emb + HD :].astype(F32), ln_gain[...], ln_bias[...])[2]
    image_high, image_low = split(image)
    narrow = all_rows[:, 0:emb]
    projected = narrow.astype(F32)
    text_scale = lax.rsqrt(jnp.sum(projected * projected, axis=1, keepdims=True) + 1e-06)
    text = projected * text_scale
    scores = (SCALE * text_scale) * (dot_rows(narrow, image_high) + dot_rows(narrow, image_low))
    grown = jnp.exp(scores)
    text_sum = jnp.sum(grown, axis=1, keepdims=True)
    image_sum = jnp.sum(grown, axis=0, keepdims=True)
    match = (lax.broadcasted_iota(jnp.int32, (count, count), 0) == pairs[...]).astype(F32)
    loss[...] = (
        jnp.sum(jnp.log(text_sum), axis=0, keepdims=True)
        + jnp.sum(jnp.log(image_sum), axis=1, keepdims=True)
        - 2.0 * jnp.sum(jnp.sum(scores * match, axis=1, keepdims=True), axis=0, keepdims=True)
    ) * (1.0 / (2.0 * count))
    dual = 0.5 * grown * (1.0 / text_sum + 1.0 / image_sum) - match
    dual_high, dual_low = split(dual)
    grad_text = SCALE * (
        dot(dual_high, image_high) + dot(dual_high, image_low) + dot(dual_low, image_high)
    )
    grad_projected = text_scale * (
        grad_text - text * jnp.sum(grad_text * text, axis=1, keepdims=True)
    )
    grad_high, grad_low = split(grad_projected)
    pooled = all_rows[:, emb : emb + HD].astype(F32).T.astype(BF16)
    wide[...] = dot(pooled, grad_high) + dot(pooled, grad_low)
    own = adapter_grad.shape[0]
    slot = pl.multiple_of(lax.rem(lax.axis_index("dp"), 4) * own, own)
    adapter_grad[...] = wide[pl.ds(slot, own), :]
    few = features.shape[0]
    chosen = (
        lax.broadcasted_iota(jnp.int32, (few, count), 1)
        == lax.axis_index(("dp", "mp")) * few + lax.broadcasted_iota(jnp.int32, (few, count), 0)
    ).astype(BF16)
    dual_own = dot_rows(chosen, dual_high) + dot_rows(chosen, dual_low)
    own_high, own_low = split(dual_own)
    text_high, text_low = split(text)
    grad_image = SCALE * (
        dot(own_high, text_high) + dot(own_high, text_low) + dot(own_low, text_high)
    )
    unit, spread, mine, scale = image_tower(
        features[...].astype(F32), ln_gain[...], ln_bias[...]
    )
    grad_normal = scale * (grad_image - mine * jnp.sum(grad_image * mine, axis=1, keepdims=True))
    grad_unit = grad_normal * ln_gain[...]
    feature_grad[...] = spread * (
        grad_unit
        - jnp.mean(grad_unit, axis=1, keepdims=True)
        - unit * jnp.mean(grad_unit * unit, axis=1, keepdims=True)
    )


def y_shift(step):
    return [(y * 2 + z, ((y + step) % 4) * 2 + z) for y in range(4) for z in range(2)]


Z_SWAP = [(m, m ^ 1) for m in range(8)]


def on_device(
    hidden,
    segment_ids,
    attn_gain,
    w_query,
    w_key,
    w_value,
    w_out,
    final_gain,
    adapter,
    features,
    ln_gain,
    ln_bias,
    pair_ids,
):
    length, width = hidden.shape
    emb_rows, emb = features.shape
    tensor_count = lax.axis_size("mp")
    seqs = lax.axis_size("dp")
    mine = lax.axis_index("mp")
    params = pltpu.CompilerParams(vmem_limit_bytes=16 * 1024 * 1024)
    roomy = pltpu.CompilerParams(vmem_limit_bytes=56 * 1024 * 1024)
    whole = pl.BlockSpec(memory_space=pltpu.VMEM)
    anywhere = pl.BlockSpec(memory_space=pl.ANY)
    far = pl.BlockSpec(memory_space=pltpu.HBM)
    small = length // 8
    cut = 2304
    q_cols = w_query.shape[1]
    kv_cols = w_key.shape[1]
    cosine, sine = rope_tables(length)
    late = jax.ShapeDtypeStruct((4 * small, width - cut), BF16)
    one = jax.ShapeDtypeStruct((2 * small, cut // 2), BF16)
    two = jax.ShapeDtypeStruct((4 * small, cut // 2), BF16)
    early = jax.ShapeDtypeStruct((2 * small, cut), BF16)
    send, keep, up_1, down_1, up_2, down_2, a_own = pl.pallas_call(
        text_kernel,
        out_shape=[late, late, two, two, one, one, early],
        in_specs=[far] * 5 + [whole, far, far, whole],
        out_specs=[anywhere] * 7,
        scratch_shapes=[
            pltpu.VMEM((length, width), BF16),
            pltpu.VMEM((width, q_cols + 2 * kv_cols), BF16),
            pltpu.VMEM((q_cols, width), BF16),
            pltpu.VMEM((2, length, HD), F32),
            pltpu.VMEM((length, q_cols + 2 * kv_cols), F32),
            pltpu.VMEM((length, q_cols), BF16),
            pltpu.VMEM((length, kv_cols), BF16),
            pltpu.VMEM((length, 2 * kv_cols), BF16),
            pltpu.VMEM((length, q_cols), BF16),
            pltpu.VMEM((length, q_cols), BF16),
            pltpu.VMEM((length, cut), BF16),
            pltpu.VMEM(late.shape, BF16),
            pltpu.VMEM(late.shape, BF16),
            pltpu.SemaphoreType.DMA((5, 4)),
            pltpu.SemaphoreType.DMA((15,)),
        ],
        compiler_params=pltpu.CompilerParams(vmem_limit_bytes=56 * 1024 * 1024),
        name="text_tower",
    )(
        hidden, w_query, w_key, w_value, w_out, attn_gain.reshape(1, width),
        jnp.asarray(cosine), jnp.asarray(sine), segment_ids,
    )
    swapped = lax.ppermute(send, "mp", Z_SWAP)
    up_1 = lax.ppermute(up_1, "mp", y_shift(1))
    down_1 = lax.ppermute(down_1, "mp", y_shift(3))
    rows = lax.dynamic_slice_in_dim(hidden, mine * small, small, 0)
    up_2, rows = lax.optimization_barrier((up_2, rows))
    up_2, down_2 = pl.pallas_call(
        pass_on_kernel,
        out_shape=[one, one],
        in_specs=[anywhere] * 4,
        out_specs=[whole] * 2,
        scratch_shapes=[pltpu.VMEM((4,) + one.shape, BF16), pltpu.SemaphoreType.DMA((4,))],
        compiler_params=roomy,
        name="pass_on",
    )(up_2, down_2, up_1, down_1)
    r_up = lax.ppermute(up_2, "mp", y_shift(1))
    r_down = lax.ppermute(down_2, "mp", y_shift(3))
    blocks = pl.pallas_call(
        swap_kernel,
        out_shape=[jax.ShapeDtypeStruct((small, width - cut), BF16)] * 4,
        in_specs=[whole] * 2 + [anywhere],
        out_specs=[whole] * 4,
        compiler_params=params,
        name="add_swapped",
    )(keep, swapped, up_2)
    q_2 = lax.ppermute(blocks[2], "mp", y_shift(2))
    q_1 = lax.ppermute(blocks[1], "mp", y_shift(1))
    q_3 = lax.ppermute(blocks[3], "mp", y_shift(3))
    weights = pl.pallas_call(
        fetch_kernel,
        out_shape=jax.ShapeDtypeStruct(adapter.shape, BF16),
        in_specs=[anywhere] * 2,
        out_specs=whole,
        scratch_shapes=[pltpu.SemaphoreType.DMA],
        compiler_params=params,
        name="fetch_weights",
    )(adapter, blocks[2])
    kept, sent = pl.pallas_call(
        fold_kernel,
        out_shape=[
            jax.ShapeDtypeStruct((small, cut), F32),
            jax.ShapeDtypeStruct((small, cut), BF16),
        ],
        in_specs=[whole] * 5 + [anywhere],
        out_specs=[whole] * 2,
        compiler_params=params,
        name="fold",
    )(a_own, up_1, down_1, r_up, r_down, weights)
    a_z = lax.ppermute(sent, "mp", Z_SWAP)
    seg = segment_ids[0]
    docs = jnp.arange(DOCS_DEV, dtype=jnp.int32)[:, None]
    counts = jnp.sum((docs == seg[None, :]).astype(F32), axis=1, keepdims=True)
    seg_rows = lax.dynamic_slice_in_dim(seg, mine * small, small, 0)
    member = (docs == seg_rows[None, :]).astype(F32) / counts
    own_cols = width // tensor_count
    chips = seqs // 2
    message = pl.pallas_call(
        pool_kernel,
        out_shape=jax.ShapeDtypeStruct((tensor_count, DOCS_DEV, emb + own_cols + HD), BF16),
        in_specs=[whole] * 11,
        out_specs=whole,
        scratch_shapes=[pltpu.VMEM((DOCS_DEV, width), BF16)],
        compiler_params=params,
        name="pool_and_project",
    )(
        rows, weights, member, final_gain.reshape(1, width), features,
        kept, a_z, blocks[0], q_1, q_2, q_3,
    )
    message = lax.all_to_all(message, "mp", 0, 0, tiled=True)
    second = pl.pallas_call(
        sum_kernel,
        out_shape=jax.ShapeDtypeStruct((chips, DOCS_DEV, 2 * emb + HD), BF16),
        in_specs=[whole],
        out_specs=whole,
        scratch_shapes=[pltpu.VMEM((DOCS_DEV, emb), F32)],
        compiler_params=params,
        name="sum_partials",
    )(message)
    second = lax.all_to_all(
        second, "dp", 0, 0, tiled=True,
        axis_index_groups=[[2 * chip + core for chip in range(chips)] for core in range(2)],
    ).reshape(chips * DOCS_DEV, 2 * emb + HD)
    other = lax.ppermute(second, "dp", [(d, d ^ 1) for d in range(seqs)])
    count = seqs * DOCS_DEV
    own = width // (seqs * tensor_count)
    loss, adapter_grad, feature_grad = pl.pallas_call(
        loss_kernel,
        out_shape=[
            jax.ShapeDtypeStruct((1, 1), F32),
            jax.ShapeDtypeStruct((own, emb), F32),
            jax.ShapeDtypeStruct((emb_rows, emb), F32),
        ],
        in_specs=[whole] * 6,
        out_specs=[whole] * 3,
        scratch_shapes=[pltpu.VMEM((count, 2 * emb + HD), BF16), pltpu.VMEM((HD, emb), F32)],
        compiler_params=params,
        name="loss_and_gradients",
    )(
        second, other, features,
        ln_gain.reshape(1, emb), ln_bias.reshape(1, emb), pair_ids.reshape(1, count),
    )
    return (loss[0, 0], adapter_grad, feature_grad)


def solution(mesh):
    return jax.shard_map(
        on_device,
        mesh=mesh,
        in_specs=(
            P("dp", None),
            P("dp", None),
            P(),
            P(None, "mp"),
            P(None, "mp"),
            P(None, "mp"),
            P("mp", None),
            P(),
            P(),
            P(("dp", "mp"), None),
            P(),
            P(),
            P(),
        ),
        out_specs=(P(), P(("dp", "mp"), None), P(("dp", "mp"), None)),
        check_vma=False,
    )
```

```python
import jax
import jax.numpy as jnp
import numpy as np
from jax import lax
from jax.experimental import pallas as pl
from jax.experimental.pallas import tpu as pltpu
from jax.sharding import PartitionSpec as P

HD = 128
DOCS_DEV = 16
SCALE = 1.0 / 0.07
EPS = 1e-05
HIGH = lax.Precision.HIGHEST
F32 = jnp.float32
BF16 = jnp.bfloat16


def rope_tables(length):
    half = HD // 2
    freq = 500000.0 ** (-np.arange(half) * 2.0 / HD)
    angle = np.arange(length)[:, None] * freq[None, :]
    cosine = np.concatenate([np.cos(angle), np.cos(angle)], axis=1)
    sine = np.concatenate([-np.sin(angle), np.sin(angle)], axis=1)
    return cosine.astype(np.float32), sine.astype(np.float32)


def dot(left, right, precision=None):
    return jnp.dot(left, right, precision=precision, preferred_element_type=F32)


def dot_rows(left, right, precision=None):
    return lax.dot_general(
        left, right, (((1,), (1,)), ((), ())), precision=precision, preferred_element_type=F32
    )


def text_kernel(
    hidden, w_query, w_key, w_value, w_out, gain, cosine, sine, seg,
    z_send, up_1, down_1, ordered_out,
    hid, w_in, w_up, table, acc, query, keys, values, att, ordered, stage, stage_send, sems, out_sems,
):
    length, width = hidden.shape
    q_local = w_query.shape[1] // HD
    parts = 4
    span = width // parts
    q_cols = w_query.shape[1]
    kv_cols = w_key.shape[1]
    copies = []
    for part in range(parts):
        rows = pl.ds(part * span, span)
        group = [
            pltpu.make_async_copy(hidden.at[:, rows], hid.at[:, rows], sems.at[part, 0]),
            pltpu.make_async_copy(
                w_query.at[rows, :], w_in.at[rows, pl.ds(0, q_cols)], sems.at[part, 1]
            ),
            pltpu.make_async_copy(
                w_key.at[rows, :], w_in.at[rows, pl.ds(q_cols, kv_cols)], sems.at[part, 2]
            ),
            pltpu.make_async_copy(
                w_value.at[rows, :], w_in.at[rows, pl.ds(q_cols + kv_cols, kv_cols)], sems.at[part, 3]
            ),
        ]
        for copy in group:
            copy.start()
        copies.append(group)
    table_copies = [
        pltpu.make_async_copy(cosine, table.at[0], sems.at[parts, 1]),
        pltpu.make_async_copy(sine, table.at[1], sems.at[parts, 2]),
    ]
    for copy in table_copies:
        copy.start()
    up_copy = pltpu.make_async_copy(w_out, w_up, sems.at[parts, 0])
    up_copy.start()
    squares = jnp.zeros((length, HD), F32)
    for part in range(parts):
        for copy in copies[part]:
            copy.wait()
        cols = slice(part * span, (part + 1) * span)
        stream = hid[:, cols].astype(F32)
        for lane in range(0, span, HD):
            piece = stream[:, lane : lane + HD]
            squares = squares + piece * piece
        scaled = (stream * gain[:, cols]).astype(BF16)
        product = dot(scaled, w_in[cols, :])
        if part == 0:
            acc[...] = product
        else:
            acc[...] += product
    norm = lax.rsqrt(jnp.sum(squares, axis=1, keepdims=True) * (1.0 / width) + EPS)
    for copy in table_copies:
        copy.wait()
    cos_t = table[0] * norm
    sin_t = table[1] * norm
    value = acc[:, q_cols : q_cols + HD]
    keys[...] = (value * cos_t + pltpu.roll(value, HD // 2, 1) * sin_t).astype(BF16)
    values[:, 0:HD] = (acc[:, q_cols + HD :] * norm).astype(BF16)
    values[:, HD:] = jnp.ones((length, HD), BF16)
    cos_t = cos_t * HD ** (-0.5)
    sin_t = sin_t * HD ** (-0.5)
    for head in range(q_local):
        lanes = slice(head * HD, (head + 1) * HD)
        value = acc[:, lanes]
        query[:, lanes] = (value * cos_t + pltpu.roll(value, HD // 2, 1) * sin_t).astype(BF16)
    block = 128
    seg_f = seg[...].astype(F32)
    for at in range(length // block):
        first = max(0, at - 1) * block
        last = (at + 1) * block
        rows = slice(at * block, last)
        seg_q = jnp.broadcast_to(seg_f[:, rows], (block, block)).T
        masks = []
        for key_at in range(first, last, block):
            seg_k = jnp.broadcast_to(seg_f[:, key_at : key_at + block], (block, block))
            live = seg_q == seg_k
            if key_at == at * block:
                live = live & (
                    lax.broadcasted_iota(jnp.int32, (block, block), 0)
                    >= lax.broadcasted_iota(jnp.int32, (block, block), 1)
                )
            masks.append(jnp.where(live, 0.0, -1e30))
        mask = masks[0] if len(masks) == 1 else jnp.concatenate(masks, axis=1)
        mask = jnp.concatenate([mask] * q_local, axis=0)
        stacked = jnp.concatenate(
            [query[rows, head * HD : (head + 1) * HD] for head in range(q_local)], axis=0
        )
        score = dot_rows(stacked, keys[first:last, :]) + mask
        weight = jnp.exp(score - jnp.max(score, axis=1, keepdims=True)).astype(BF16)
        result = dot(weight, values[first:last, :])
        result = (result[:, 0:HD] / result[:, HD:]).astype(BF16)
        for head in range(q_local):
            att[rows, head * HD : (head + 1) * HD] = result[head * block : (head + 1) * block]
    index = lax.axis_index("mp")
    y, z = index // 2, lax.rem(index, 2)
    small = length // 8
    for step in range(4):
        base = lax.rem(y + step, 4) * 2
        mine = pl.multiple_of((base + z) * small, small)
        other = pl.multiple_of((base + 1 - z) * small, small)
        at = step * small
        ordered[pl.ds(at, small), :] = att[pl.ds(mine, small), :]
        ordered[pl.ds(4 * small + at, small), :] = att[pl.ds(other, small), :]
    up_copy.wait()
    side = up_1.shape[1]
    cut = 2 * side
    sends = []

    def ship(source, target):
        send = pltpu.make_async_copy(source, target, out_sems.at[len(sends)])
        send.start()
        sends.append(send)

    for start, stop in pieces(cut, width):
        stage_send[:, start - cut : stop - cut] = dot(
            ordered[4 * small :, :], w_up[:, start:stop]
        ).astype(BF16)
    ship(stage_send, z_send)
    ship(ordered, ordered_out)
    far = jnp.concatenate(
        [ordered[2 * small : 3 * small, :], ordered[6 * small : 7 * small, :]], axis=0
    )
    for start, stop in pieces(0, cut):
        stage[:, start:stop] = dot(far, w_up[:, start:stop]).astype(BF16)
    ship(stage.at[:, pl.ds(0, side)], up_1)
    ship(stage.at[:, pl.ds(side, side)], down_1)
    for send in sends:
        send.wait()


def pieces(first, last, chunk=512):
    edges = list(range(first, last - chunk + 1, chunk)) + [last]
    return list(zip(edges[:-1], edges[1:]))


def rest_kernel(ordered, w_out, up_near, down_near, up_2, down_2, own, keep):
    side = up_2.shape[1]
    cut = 2 * side
    width = w_out.shape[1]
    small = keep.shape[0] // 4
    wide = 2 * small
    rows = jnp.concatenate(
        [
            ordered[(4 * half + step) * small : (4 * half + step + 1) * small, :]
            for step in (1, 3, 0)
            for half in range(2)
        ],
        axis=0,
    )
    for base, near, far in ((0, (down_near, 1), (up_2, 0)), (side, (up_near, 0), (down_2, 1))):
        for start, stop in pieces(base, base + side):
            result = dot(rows, w_out[:, start:stop]).astype(BF16)
            cols = slice(start - base, stop - base)
            for ref, at in (near, far):
                ref[:, cols] = result[at * wide : (at + 1) * wide]
            own[:, start:stop] = result[2 * wide :]
    for start, stop in pieces(cut, width):
        keep[:, start - cut : stop - cut] = dot(
            ordered[0 : 4 * small, :], w_out[:, start:stop]
        ).astype(BF16)


def add(left, right):
    return (left.astype(F32) + right.astype(F32)).astype(BF16)


def pass_on_kernel(up_2, down_2, up_1, down_1, up, down):
    up[...] = add(up_2[...], up_1[...])
    down[...] = add(down_2[...], down_1[...])


def swap_kernel(keep, swapped, after, block_0, block_1, block_2, block_3):
    size = block_0.shape[0]
    for step, block in enumerate((block_0, block_1, block_2, block_3)):
        rows = slice(step * size, (step + 1) * size)
        block[...] = add(keep[rows, :], swapped[rows, :])


def fold_kernel(own, up_near, down_near, up_2, down_2, after, kept, sent):
    small = kept.shape[0]
    total = ring_sum(own, up_near, down_near, up_2, down_2)
    kept[...] = total[:small]
    sent[...] = total[small:].astype(BF16)


def fetch_kernel(adapter, after, weights, sem):
    copy = pltpu.make_async_copy(adapter, weights, sem)
    copy.start()
    copy.wait()


def ring_sum(own, up_near, down_near, up_2, down_2):
    width = own.shape[1]
    side = width // 2
    left = own[:, 0:side].astype(F32) + down_near[...].astype(F32) + up_2[...].astype(F32)
    right = own[:, side:].astype(F32) + up_near[...].astype(F32) + down_2[...].astype(F32)
    return jnp.concatenate([left, right], axis=1)


def pool_kernel(
    rows, adapter, member, gain, features, kept, a_z, b_own, b_1, b_2, b_3, message, doc,
):
    small, width = rows.shape
    left = kept[...] + a_z[...].astype(F32)
    right = b_own[...].astype(F32) + b_1[...].astype(F32)
    right = right + b_2[...].astype(F32) + b_3[...].astype(F32)
    residual = jnp.concatenate([left, right], axis=1) + rows[...].astype(F32)
    norm = lax.rsqrt(jnp.sum(residual * residual, axis=1, keepdims=True) * (1.0 / width) + EPS)
    final = residual * norm * gain[...]
    means = dot(member[...], final, HIGH)
    doc[...] = means.astype(BF16)
    emb = adapter.shape[1]
    projected = dot(doc[...], adapter[...])
    projected = projected.astype(BF16)
    own = 32
    seqs = 16
    lane = lax.broadcasted_iota(jnp.int32, (DOCS_DEV, HD), 1) // own
    for peer in range(8):
        message[peer, :, 0:emb] = projected
        for group in range(seqs // 4):
            tile = None
            for slot in range(4):
                at = (2 * (group * 4 + slot) + peer // 4) * HD
                piece = means[:, at : at + HD]
                shift = ((slot - peer % 4) * own) % HD
                if shift:
                    piece = pltpu.roll(piece, shift, 1)
                tile = piece if tile is None else jnp.where(lane == slot, piece, tile)
            message[peer, :, emb + group * HD : emb + (group + 1) * HD] = tile.astype(BF16)
    image_rows = features[...].astype(F32)
    per_row = emb // HD
    lined = jnp.concatenate(
        [
            image_rows[row : row + 1, at * HD : (at + 1) * HD]
            for row in range(features.shape[0])
            for at in range(per_row)
        ],
        axis=0,
    ).astype(BF16)
    for peer in range(8):
        message[peer, :, emb + seqs * own :] = lined


def sum_kernel(message, second, images):
    emb = images.shape[1]
    cut = message.shape[2] - HD
    total = message[0, :, 0:cut].astype(F32)
    for peer in range(1, message.shape[0]):
        total = total + message[peer, :, 0:cut].astype(F32)
    total = total.astype(BF16)
    per_row = emb // HD
    for peer in range(message.shape[0]):
        lined = message[peer, :, cut:].astype(F32)
        for at in range(lined.shape[0]):
            row = peer * (lined.shape[0] // per_row) + at // per_row
            lane = (at % per_row) * HD
            images[row : row + 1, lane : lane + HD] = lined[at : at + 1, :]
    image_rows = images[...].astype(BF16)
    for chip in range(second.shape[0]):
        second[chip, :, 0:emb] = total[:, 0:emb]
        at = emb + (chip // 2) * HD
        second[chip, :, emb : emb + HD] = total[:, at : at + HD]
        second[chip, :, emb + HD :] = image_rows


def image_tower(values, gain, shift):
    center = values - jnp.mean(values, axis=1, keepdims=True)
    spread = lax.rsqrt(jnp.mean(center * center, axis=1, keepdims=True) + EPS)
    unit = center * spread
    normal = unit * gain + shift
    scale = lax.rsqrt(jnp.sum(normal * normal, axis=1, keepdims=True) + 1e-06)
    return unit, spread, normal * scale, scale


def split(value):
    high = value.astype(BF16)
    return high, (value - high.astype(F32)).astype(BF16)


def loss_kernel(
    same, other, features, ln_gain, ln_bias, pairs, loss, adapter_grad, feature_grad, all_rows, wide
):
    count = all_rows.shape[0]
    emb = features.shape[1]
    core = lax.rem(lax.axis_index("dp"), 2)
    for chip in range(count // (2 * DOCS_DEV)):
        rows = slice(chip * DOCS_DEV, (chip + 1) * DOCS_DEV)
        for ref, at in ((same, core), (other, 1 - core)):
            start = pl.multiple_of((2 * chip + at) * DOCS_DEV, DOCS_DEV)
            all_rows[pl.ds(start, DOCS_DEV), :] = ref[rows, :]
    image = image_tower(all_rows[:, emb + HD :].astype(F32), ln_gain[...], ln_bias[...])[2]
    image_high, image_low = split(image)
    narrow = all_rows[:, 0:emb]
    projected = narrow.astype(F32)
    text_scale = lax.rsqrt(jnp.sum(projected * projected, axis=1, keepdims=True) + 1e-06)
    text = projected * text_scale
    scores = (SCALE * text_scale) * (dot_rows(narrow, image_high) + dot_rows(narrow, image_low))
    grown = jnp.exp(scores)
    text_sum = jnp.sum(grown, axis=1, keepdims=True)
    image_sum = jnp.sum(grown, axis=0, keepdims=True)
    match = (lax.broadcasted_iota(jnp.int32, (count, count), 0) == pairs[...]).astype(F32)
    loss[...] = (
        jnp.sum(jnp.log(text_sum), axis=0, keepdims=True)
        + jnp.sum(jnp.log(image_sum), axis=1, keepdims=True)
        - 2.0 * jnp.sum(jnp.sum(scores * match, axis=1, keepdims=True), axis=0, keepdims=True)
    ) * (1.0 / (2.0 * count))
    dual = 0.5 * grown * (1.0 / text_sum + 1.0 / image_sum) - match
    dual_high, dual_low = split(dual)
    grad_text = SCALE * (
        dot(dual_high, image_high) + dot(dual_high, image_low) + dot(dual_low, image_high)
    )
    grad_projected = text_scale * (
        grad_text - text * jnp.sum(grad_text * text, axis=1, keepdims=True)
    )
    grad_high, grad_low = split(grad_projected)
    pooled = all_rows[:, emb : emb + HD].astype(F32).T.astype(BF16)
    wide[...] = dot(pooled, grad_high) + dot(pooled, grad_low)
    own = adapter_grad.shape[0]
    slot = pl.multiple_of(lax.rem(lax.axis_index("dp"), 4) * own, own)
    adapter_grad[...] = wide[pl.ds(slot, own), :]
    few = features.shape[0]
    chosen = (
        lax.broadcasted_iota(jnp.int32, (few, count), 1)
        == lax.axis_index(("dp", "mp")) * few + lax.broadcasted_iota(jnp.int32, (few, count), 0)
    ).astype(BF16)
    dual_own = dot_rows(chosen, dual_high) + dot_rows(chosen, dual_low)
    own_high, own_low = split(dual_own)
    text_high, text_low = split(text)
    grad_image = SCALE * (
        dot(own_high, text_high) + dot(own_high, text_low) + dot(own_low, text_high)
    )
    unit, spread, mine, scale = image_tower(
        features[...].astype(F32), ln_gain[...], ln_bias[...]
    )
    grad_normal = scale * (grad_image - mine * jnp.sum(grad_image * mine, axis=1, keepdims=True))
    grad_unit = grad_normal * ln_gain[...]
    feature_grad[...] = spread * (
        grad_unit
        - jnp.mean(grad_unit, axis=1, keepdims=True)
        - unit * jnp.mean(grad_unit * unit, axis=1, keepdims=True)
    )


def y_shift(step):
    return [(y * 2 + z, ((y + step) % 4) * 2 + z) for y in range(4) for z in range(2)]


Z_SWAP = [(m, m ^ 1) for m in range(8)]


def on_device(
    hidden,
    segment_ids,
    attn_gain,
    w_query,
    w_key,
    w_value,
    w_out,
    final_gain,
    adapter,
    features,
    ln_gain,
    ln_bias,
    pair_ids,
):
    length, width = hidden.shape
    emb_rows, emb = features.shape
    tensor_count = lax.axis_size("mp")
    seqs = lax.axis_size("dp")
    mine = lax.axis_index("mp")
    params = pltpu.CompilerParams(vmem_limit_bytes=16 * 1024 * 1024)
    roomy = pltpu.CompilerParams(vmem_limit_bytes=56 * 1024 * 1024)
    whole = pl.BlockSpec(memory_space=pltpu.VMEM)
    anywhere = pl.BlockSpec(memory_space=pl.ANY)
    far = pl.BlockSpec(memory_space=pltpu.HBM)
    small = length // 8
    cut = 2304
    q_cols = w_query.shape[1]
    kv_cols = w_key.shape[1]
    cosine, sine = rope_tables(length)
    late = jax.ShapeDtypeStruct((4 * small, width - cut), BF16)
    one = jax.ShapeDtypeStruct((2 * small, cut // 2), BF16)
    early = jax.ShapeDtypeStruct((2 * small, cut), BF16)
    send, up_1, down_1, ordered = pl.pallas_call(
        text_kernel,
        out_shape=[late, one, one, jax.ShapeDtypeStruct((length, q_cols), BF16)],
        in_specs=[far] * 5 + [whole, far, far, whole],
        out_specs=[anywhere] * 4,
        scratch_shapes=[
            pltpu.VMEM((length, width), BF16),
            pltpu.VMEM((width, q_cols + 2 * kv_cols), BF16),
            pltpu.VMEM((q_cols, width), BF16),
            pltpu.VMEM((2, length, HD), F32),
            pltpu.VMEM((length, q_cols + 2 * kv_cols), F32),
            pltpu.VMEM((length, q_cols), BF16),
            pltpu.VMEM((length, kv_cols), BF16),
            pltpu.VMEM((length, 2 * kv_cols), BF16),
            pltpu.VMEM((length, q_cols), BF16),
            pltpu.VMEM((length, q_cols), BF16),
            pltpu.VMEM((2 * small, cut), BF16),
            pltpu.VMEM(late.shape, BF16),
            pltpu.SemaphoreType.DMA((5, 4)),
            pltpu.SemaphoreType.DMA((4,)),
        ],
        compiler_params=pltpu.CompilerParams(vmem_limit_bytes=56 * 1024 * 1024),
        name="text_tower",
    )(
        hidden, w_query, w_key, w_value, w_out, attn_gain.reshape(1, width),
        jnp.asarray(cosine), jnp.asarray(sine), segment_ids,
    )
    swapped = lax.ppermute(send, "mp", Z_SWAP)
    up_1 = lax.ppermute(up_1, "mp", y_shift(1))
    down_1 = lax.ppermute(down_1, "mp", y_shift(3))
    up_near, down_near, up_2, down_2, a_own, keep = pl.pallas_call(
        rest_kernel,
        out_shape=[one] * 4 + [early, late],
        in_specs=[whole] * 2,
        out_specs=[whole] * 6,
        compiler_params=pltpu.CompilerParams(vmem_limit_bytes=24 * 1024 * 1024),
        cost_estimate=pl.CostEstimate(
            flops=length * q_cols * width, bytes_accessed=4 * q_cols * width, transcendentals=0
        ),
        name="other_terms",
    )(ordered, w_out)
    up_near = lax.ppermute(up_near, "mp", y_shift(1))
    down_near = lax.ppermute(down_near, "mp", y_shift(3))
    rows = lax.dynamic_slice_in_dim(hidden, mine * small, small, 0)
    up_2, rows = lax.optimization_barrier((up_2, rows))
    up_2, down_2 = pl.pallas_call(
        pass_on_kernel,
        out_shape=[one, one],
        in_specs=[whole] * 4,
        out_specs=[whole] * 2,
        compiler_params=params,
        name="pass_on",
    )(up_2, down_2, up_1, down_1)
    r_up = lax.ppermute(up_2, "mp", y_shift(1))
    r_down = lax.ppermute(down_2, "mp", y_shift(3))
    weights = pl.pallas_call(
        fetch_kernel,
        out_shape=jax.ShapeDtypeStruct(adapter.shape, BF16),
        in_specs=[anywhere] * 2,
        out_specs=whole,
        scratch_shapes=[pltpu.SemaphoreType.DMA],
        compiler_params=params,
        name="fetch_weights",
    )(adapter, up_2)
    blocks = pl.pallas_call(
        swap_kernel,
        out_shape=[jax.ShapeDtypeStruct((small, width - cut), BF16)] * 4,
        in_specs=[whole] * 2 + [anywhere],
        out_specs=[whole] * 4,
        compiler_params=params,
        name="add_swapped",
    )(keep, swapped, weights)
    q_2 = lax.ppermute(blocks[2], "mp", y_shift(2))
    q_1 = lax.ppermute(blocks[1], "mp", y_shift(1))
    q_3 = lax.ppermute(blocks[3], "mp", y_shift(3))
    kept, sent = pl.pallas_call(
        fold_kernel,
        out_shape=[
            jax.ShapeDtypeStruct((small, cut), F32),
            jax.ShapeDtypeStruct((small, cut), BF16),
        ],
        in_specs=[whole] * 5 + [anywhere],
        out_specs=[whole] * 2,
        compiler_params=params,
        name="fold",
    )(a_own, up_near, down_near, r_up, r_down, blocks[2])
    a_z = lax.ppermute(sent, "mp", Z_SWAP)
    seg = segment_ids[0]
    docs = jnp.arange(DOCS_DEV, dtype=jnp.int32)[:, None]
    counts = jnp.sum((docs == seg[None, :]).astype(F32), axis=1, keepdims=True)
    seg_rows = lax.dynamic_slice_in_dim(seg, mine * small, small, 0)
    member = (docs == seg_rows[None, :]).astype(F32) / counts
    own_cols = width // tensor_count
    chips = seqs // 2
    message = pl.pallas_call(
        pool_kernel,
        out_shape=jax.ShapeDtypeStruct((tensor_count, DOCS_DEV, emb + own_cols + HD), BF16),
        in_specs=[whole] * 11,
        out_specs=whole,
        scratch_shapes=[pltpu.VMEM((DOCS_DEV, width), BF16)],
        compiler_params=params,
        name="pool_and_project",
    )(
        rows, weights, member, final_gain.reshape(1, width), features,
        kept, a_z, blocks[0], q_1, q_2, q_3,
    )
    message = lax.all_to_all(message, "mp", 0, 0, tiled=True)
    second = pl.pallas_call(
        sum_kernel,
        out_shape=jax.ShapeDtypeStruct((chips, DOCS_DEV, 2 * emb + HD), BF16),
        in_specs=[whole],
        out_specs=whole,
        scratch_shapes=[pltpu.VMEM((DOCS_DEV, emb), F32)],
        compiler_params=params,
        name="sum_partials",
    )(message)
    second = lax.all_to_all(
        second, "dp", 0, 0, tiled=True,
        axis_index_groups=[[2 * chip + core for chip in range(chips)] for core in range(2)],
    ).reshape(chips * DOCS_DEV, 2 * emb + HD)
    other = lax.ppermute(second, "dp", [(d, d ^ 1) for d in range(seqs)])
    count = seqs * DOCS_DEV
    own = width // (seqs * tensor_count)
    loss, adapter_grad, feature_grad = pl.pallas_call(
        loss_kernel,
        out_shape=[
            jax.ShapeDtypeStruct((1, 1), F32),
            jax.ShapeDtypeStruct((own, emb), F32),
            jax.ShapeDtypeStruct((emb_rows, emb), F32),
        ],
        in_specs=[whole] * 6,
        out_specs=[whole] * 3,
        scratch_shapes=[pltpu.VMEM((count, 2 * emb + HD), BF16), pltpu.VMEM((HD, emb), F32)],
        compiler_params=params,
        name="loss_and_gradients",
    )(
        second, other, features,
        ln_gain.reshape(1, emb), ln_bias.reshape(1, emb), pair_ids.reshape(1, count),
    )
    return (loss[0, 0], adapter_grad, feature_grad)


def solution(mesh):
    return jax.shard_map(
        on_device,
        mesh=mesh,
        in_specs=(
            P("dp", None),
            P("dp", None),
            P(),
            P(None, "mp"),
            P(None, "mp"),
            P(None, "mp"),
            P("mp", None),
            P(),
            P(),
            P(("dp", "mp"), None),
            P(),
            P(),
            P(),
        ),
        out_specs=(P(), P(("dp", "mp"), None), P(("dp", "mp"), None)),
        check_vma=False,
    )
```

```python
import jax
import jax.numpy as jnp
import numpy as np
from jax import lax
from jax.experimental import pallas as pl
from jax.experimental.pallas import tpu as pltpu
from jax.sharding import PartitionSpec as P

HD = 128
DOCS_DEV = 16
SCALE = 1.0 / 0.07
EPS = 1e-05
HIGH = lax.Precision.HIGHEST
F32 = jnp.float32
BF16 = jnp.bfloat16


def rope_tables(length):
    half = HD // 2
    freq = 500000.0 ** (-np.arange(half) * 2.0 / HD)
    angle = np.arange(length)[:, None] * freq[None, :]
    cosine = np.concatenate([np.cos(angle), np.cos(angle)], axis=1)
    sine = np.concatenate([-np.sin(angle), np.sin(angle)], axis=1)
    return cosine.astype(np.float32), sine.astype(np.float32)


def dot(left, right, precision=None):
    return jnp.dot(left, right, precision=precision, preferred_element_type=F32)


def dot_rows(left, right, precision=None):
    return lax.dot_general(
        left, right, (((1,), (1,)), ((), ())), precision=precision, preferred_element_type=F32
    )


def text_kernel(
    hidden, w_query, w_key, w_value, w_out, gain, cosine, sine, seg,
    z_send, up_1, down_1, ordered_out,
    hid, w_in, w_up, table, acc, query, keys, values, att, ordered, stage, stage_send, sems, out_sems,
):
    length, width = hidden.shape
    q_local = w_query.shape[1] // HD
    parts = 4
    span = width // parts
    q_cols = w_query.shape[1]
    kv_cols = w_key.shape[1]
    copies = []
    for part in range(parts):
        rows = pl.ds(part * span, span)
        group = [
            pltpu.make_async_copy(hidden.at[:, rows], hid.at[:, rows], sems.at[part, 0]),
            pltpu.make_async_copy(
                w_query.at[rows, :], w_in.at[rows, pl.ds(0, q_cols)], sems.at[part, 1]
            ),
            pltpu.make_async_copy(
                w_key.at[rows, :], w_in.at[rows, pl.ds(q_cols, kv_cols)], sems.at[part, 2]
            ),
            pltpu.make_async_copy(
                w_value.at[rows, :], w_in.at[rows, pl.ds(q_cols + kv_cols, kv_cols)], sems.at[part, 3]
            ),
        ]
        for copy in group:
            copy.start()
        copies.append(group)
    table_copies = [
        pltpu.make_async_copy(cosine, table.at[0], sems.at[parts, 1]),
        pltpu.make_async_copy(sine, table.at[1], sems.at[parts, 2]),
    ]
    for copy in table_copies:
        copy.start()
    up_copy = pltpu.make_async_copy(w_out, w_up, sems.at[parts, 0])
    up_copy.start()
    squares = jnp.zeros((length, HD), F32)
    for part in range(parts):
        for copy in copies[part]:
            copy.wait()
        cols = slice(part * span, (part + 1) * span)
        stream = hid[:, cols].astype(F32)
        for lane in range(0, span, HD):
            piece = stream[:, lane : lane + HD]
            squares = squares + piece * piece
        scaled = (stream * gain[:, cols]).astype(BF16)
        product = dot(scaled, w_in[cols, :])
        if part == 0:
            acc[...] = product
        else:
            acc[...] += product
    norm = lax.rsqrt(jnp.sum(squares, axis=1, keepdims=True) * (1.0 / width) + EPS)
    for copy in table_copies:
        copy.wait()
    cos_t = table[0] * norm
    sin_t = table[1] * norm
    value = acc[:, q_cols : q_cols + HD]
    keys[...] = (value * cos_t + pltpu.roll(value, HD // 2, 1) * sin_t).astype(BF16)
    values[:, 0:HD] = (acc[:, q_cols + HD :] * norm).astype(BF16)
    values[:, HD:] = jnp.ones((length, HD), BF16)
    cos_t = cos_t * HD ** (-0.5)
    sin_t = sin_t * HD ** (-0.5)
    for head in range(q_local):
        lanes = slice(head * HD, (head + 1) * HD)
        value = acc[:, lanes]
        query[:, lanes] = (value * cos_t + pltpu.roll(value, HD // 2, 1) * sin_t).astype(BF16)
    block = 128
    seg_f = seg[...].astype(F32)
    for at in range(length // block):
        first = max(0, at - 1) * block
        last = (at + 1) * block
        rows = slice(at * block, last)
        seg_q = jnp.broadcast_to(seg_f[:, rows], (block, block)).T
        masks = []
        for key_at in range(first, last, block):
            seg_k = jnp.broadcast_to(seg_f[:, key_at : key_at + block], (block, block))
            live = seg_q == seg_k
            if key_at == at * block:
                live = live & (
                    lax.broadcasted_iota(jnp.int32, (block, block), 0)
                    >= lax.broadcasted_iota(jnp.int32, (block, block), 1)
                )
            masks.append(jnp.where(live, 0.0, -1e30))
        mask = masks[0] if len(masks) == 1 else jnp.concatenate(masks, axis=1)
        mask = jnp.concatenate([mask] * q_local, axis=0)
        stacked = jnp.concatenate(
            [query[rows, head * HD : (head + 1) * HD] for head in range(q_local)], axis=0
        )
        score = dot_rows(stacked, keys[first:last, :]) + mask
        weight = jnp.exp(score - jnp.max(score, axis=1, keepdims=True)).astype(BF16)
        result = dot(weight, values[first:last, :])
        result = (result[:, 0:HD] / result[:, HD:]).astype(BF16)
        for head in range(q_local):
            att[rows, head * HD : (head + 1) * HD] = result[head * block : (head + 1) * block]
    index = lax.axis_index("mp")
    y, z = index // 2, lax.rem(index, 2)
    small = length // 8
    for step in range(4):
        base = lax.rem(y + step, 4) * 2
        mine = pl.multiple_of((base + z) * small, small)
        other = pl.multiple_of((base + 1 - z) * small, small)
        at = step * small
        ordered[pl.ds(at, small), :] = att[pl.ds(mine, small), :]
        ordered[pl.ds(4 * small + at, small), :] = att[pl.ds(other, small), :]
    up_copy.wait()
    side = up_1.shape[1]
    cut = 2 * side
    sends = []

    def ship(source, target):
        send = pltpu.make_async_copy(source, target, out_sems.at[len(sends)])
        send.start()
        sends.append(send)

    for start, stop in pieces(cut, width):
        stage_send[:, start - cut : stop - cut] = dot(
            ordered[4 * small :, :], w_up[:, start:stop]
        ).astype(BF16)
    ship(stage_send, z_send)
    ship(ordered, ordered_out)
    far = jnp.concatenate(
        [ordered[2 * small : 3 * small, :], ordered[6 * small : 7 * small, :]], axis=0
    )
    for start, stop in pieces(0, cut):
        stage[:, start:stop] = dot(far, w_up[:, start:stop]).astype(BF16)
    ship(stage.at[:, pl.ds(0, side)], up_1)
    ship(stage.at[:, pl.ds(side, side)], down_1)
    for send in sends:
        send.wait()


def pieces(first, last, chunk=512):
    edges = list(range(first, last - chunk + 1, chunk)) + [last]
    return list(zip(edges[:-1], edges[1:]))


def rest_kernel(
    ordered, w_out, features, ln_gain, ln_bias, up_near, down_near, up_2, down_2, own, keep, lined
):
    image_rows = image_tower(features[...].astype(F32), ln_gain[...], ln_bias[...])[2]
    per_row = features.shape[1] // HD
    lined[...] = jnp.concatenate(
        [
            image_rows[row : row + 1, at * HD : (at + 1) * HD]
            for row in range(features.shape[0])
            for at in range(per_row)
        ],
        axis=0,
    ).astype(BF16)
    side = up_2.shape[1]
    cut = 2 * side
    width = w_out.shape[1]
    small = keep.shape[0] // 4
    wide = 2 * small
    rows = jnp.concatenate(
        [
            ordered[(4 * half + step) * small : (4 * half + step + 1) * small, :]
            for step in (1, 3, 0)
            for half in range(2)
        ],
        axis=0,
    )
    for base, near, far in ((0, (down_near, 1), (up_2, 0)), (side, (up_near, 0), (down_2, 1))):
        for start, stop in pieces(base, base + side):
            result = dot(rows, w_out[:, start:stop]).astype(BF16)
            cols = slice(start - base, stop - base)
            for ref, at in (near, far):
                ref[:, cols] = result[at * wide : (at + 1) * wide]
            own[:, start:stop] = result[2 * wide :]
    for start, stop in pieces(cut, width):
        keep[:, start - cut : stop - cut] = dot(
            ordered[0 : 4 * small, :], w_out[:, start:stop]
        ).astype(BF16)


def add(left, right):
    return (left.astype(F32) + right.astype(F32)).astype(BF16)


def pass_on_kernel(up_2, down_2, up_1, down_1, up, down):
    up[...] = add(up_2[...], up_1[...])
    down[...] = add(down_2[...], down_1[...])


def swap_kernel(keep, swapped, after, block_0, block_1, block_2, block_3):
    size = block_0.shape[0]
    for step, block in enumerate((block_0, block_1, block_2, block_3)):
        rows = slice(step * size, (step + 1) * size)
        block[...] = add(keep[rows, :], swapped[rows, :])


def fold_kernel(own, up_near, down_near, up_2, down_2, after, kept, sent):
    small = kept.shape[0]
    total = ring_sum(own, up_near, down_near, up_2, down_2)
    kept[...] = total[:small]
    sent[...] = total[small:].astype(BF16)


def fetch_kernel(adapter, after, weights, sem):
    copy = pltpu.make_async_copy(adapter, weights, sem)
    copy.start()
    copy.wait()


def ring_sum(own, up_near, down_near, up_2, down_2):
    width = own.shape[1]
    side = width // 2
    left = own[:, 0:side].astype(F32) + down_near[...].astype(F32) + up_2[...].astype(F32)
    right = own[:, side:].astype(F32) + up_near[...].astype(F32) + down_2[...].astype(F32)
    return jnp.concatenate([left, right], axis=1)


def pool_kernel(
    rows, adapter, member, gain, lined, kept, a_z, b_own, b_1, b_2, b_3, message, doc,
):
    small, width = rows.shape
    left = kept[...] + a_z[...].astype(F32)
    right = b_own[...].astype(F32) + b_1[...].astype(F32)
    right = right + b_2[...].astype(F32) + b_3[...].astype(F32)
    residual = jnp.concatenate([left, right], axis=1) + rows[...].astype(F32)
    norm = lax.rsqrt(jnp.sum(residual * residual, axis=1, keepdims=True) * (1.0 / width) + EPS)
    final = residual * norm * gain[...]
    means = dot(member[...], final, HIGH)
    doc[...] = means.astype(BF16)
    emb = adapter.shape[1]
    projected = dot(doc[...], adapter[...])
    projected = projected.astype(BF16)
    own = 32
    seqs = 16
    lane = lax.broadcasted_iota(jnp.int32, (DOCS_DEV, HD), 1) // own
    for peer in range(8):
        message[peer, :, 0:emb] = projected
        for group in range(seqs // 4):
            tile = None
            for slot in range(4):
                at = (2 * (group * 4 + slot) + peer // 4) * HD
                piece = means[:, at : at + HD]
                shift = ((slot - peer % 4) * own) % HD
                if shift:
                    piece = pltpu.roll(piece, shift, 1)
                tile = piece if tile is None else jnp.where(lane == slot, piece, tile)
            message[peer, :, emb + group * HD : emb + (group + 1) * HD] = tile.astype(BF16)
    for peer in range(8):
        message[peer, :, emb + seqs * own :] = lined[...]


def sum_kernel(message, second, images):
    emb = images.shape[1]
    cut = message.shape[2] - HD
    total = message[0, :, 0:cut].astype(F32)
    for peer in range(1, message.shape[0]):
        total = total + message[peer, :, 0:cut].astype(F32)
    total = total.astype(BF16)
    per_row = emb // HD
    for peer in range(message.shape[0]):
        lined = message[peer, :, cut:].astype(F32)
        for at in range(lined.shape[0]):
            row = peer * (lined.shape[0] // per_row) + at // per_row
            lane = (at % per_row) * HD
            images[row : row + 1, lane : lane + HD] = lined[at : at + 1, :]
    image_rows = images[...].astype(BF16)
    for chip in range(second.shape[0]):
        second[chip, :, 0:emb] = total[:, 0:emb]
        at = emb + (chip // 2) * HD
        second[chip, :, emb : emb + HD] = total[:, at : at + HD]
        second[chip, :, emb + HD :] = image_rows


def image_tower(values, gain, shift):
    center = values - jnp.mean(values, axis=1, keepdims=True)
    spread = lax.rsqrt(jnp.mean(center * center, axis=1, keepdims=True) + EPS)
    unit = center * spread
    normal = unit * gain + shift
    scale = lax.rsqrt(jnp.sum(normal * normal, axis=1, keepdims=True) + 1e-06)
    return unit, spread, normal * scale, scale


def split(value):
    high = value.astype(BF16)
    return high, (value - high.astype(F32)).astype(BF16)


def loss_kernel(
    same, other, features, ln_gain, ln_bias, pairs, loss, adapter_grad, feature_grad, all_rows, wide
):
    count = all_rows.shape[0]
    emb = features.shape[1]
    core = lax.rem(lax.axis_index("dp"), 2)
    for chip in range(count // (2 * DOCS_DEV)):
        rows = slice(chip * DOCS_DEV, (chip + 1) * DOCS_DEV)
        for ref, at in ((same, core), (other, 1 - core)):
            start = pl.multiple_of((2 * chip + at) * DOCS_DEV, DOCS_DEV)
            all_rows[pl.ds(start, DOCS_DEV), :] = ref[rows, :]
    image = all_rows[:, emb + HD :]
    narrow = all_rows[:, 0:emb]
    projected = narrow.astype(F32)
    text_scale = lax.rsqrt(jnp.sum(projected * projected, axis=1, keepdims=True) + 1e-06)
    text = projected * text_scale
    scores = (SCALE * text_scale) * dot_rows(narrow, image)
    grown = jnp.exp(scores)
    text_sum = jnp.sum(grown, axis=1, keepdims=True)
    image_sum = jnp.sum(grown, axis=0, keepdims=True)
    match = (lax.broadcasted_iota(jnp.int32, (count, count), 0) == pairs[...]).astype(F32)
    loss[...] = (
        jnp.sum(jnp.log(text_sum), axis=0, keepdims=True)
        + jnp.sum(jnp.log(image_sum), axis=1, keepdims=True)
        - 2.0 * jnp.sum(jnp.sum(scores * match, axis=1, keepdims=True), axis=0, keepdims=True)
    ) * (1.0 / (2.0 * count))
    dual = 0.5 * grown * (1.0 / text_sum + 1.0 / image_sum) - match
    dual_high, dual_low = split(dual)
    grad_text = SCALE * (dot(dual_high, image) + dot(dual_low, image))
    grad_projected = text_scale * (
        grad_text - text * jnp.sum(grad_text * text, axis=1, keepdims=True)
    )
    grad_high, grad_low = split(grad_projected)
    pooled = all_rows[:, emb : emb + HD].astype(F32).T.astype(BF16)
    wide[...] = dot(pooled, grad_high) + dot(pooled, grad_low)
    own = adapter_grad.shape[0]
    slot = pl.multiple_of(lax.rem(lax.axis_index("dp"), 4) * own, own)
    adapter_grad[...] = wide[pl.ds(slot, own), :]
    few = features.shape[0]
    chosen = (
        lax.broadcasted_iota(jnp.int32, (few, count), 1)
        == lax.axis_index(("dp", "mp")) * few + lax.broadcasted_iota(jnp.int32, (few, count), 0)
    ).astype(BF16)
    dual_own = dot_rows(chosen, dual_high) + dot_rows(chosen, dual_low)
    own_high, own_low = split(dual_own)
    text_high, text_low = split(text)
    grad_image = SCALE * (
        dot(own_high, text_high) + dot(own_high, text_low) + dot(own_low, text_high)
    )
    unit, spread, mine, scale = image_tower(
        features[...].astype(F32), ln_gain[...], ln_bias[...]
    )
    grad_normal = scale * (grad_image - mine * jnp.sum(grad_image * mine, axis=1, keepdims=True))
    grad_unit = grad_normal * ln_gain[...]
    feature_grad[...] = spread * (
        grad_unit
        - jnp.mean(grad_unit, axis=1, keepdims=True)
        - unit * jnp.mean(grad_unit * unit, axis=1, keepdims=True)
    )


def y_shift(step):
    return [(y * 2 + z, ((y + step) % 4) * 2 + z) for y in range(4) for z in range(2)]


Z_SWAP = [(m, m ^ 1) for m in range(8)]


def on_device(
    hidden,
    segment_ids,
    attn_gain,
    w_query,
    w_key,
    w_value,
    w_out,
    final_gain,
    adapter,
    features,
    ln_gain,
    ln_bias,
    pair_ids,
):
    length, width = hidden.shape
    emb_rows, emb = features.shape
    tensor_count = lax.axis_size("mp")
    seqs = lax.axis_size("dp")
    mine = lax.axis_index("mp")
    params = pltpu.CompilerParams(vmem_limit_bytes=16 * 1024 * 1024)
    roomy = pltpu.CompilerParams(vmem_limit_bytes=56 * 1024 * 1024)
    whole = pl.BlockSpec(memory_space=pltpu.VMEM)
    anywhere = pl.BlockSpec(memory_space=pl.ANY)
    far = pl.BlockSpec(memory_space=pltpu.HBM)
    small = length // 8
    cut = 2304
    q_cols = w_query.shape[1]
    kv_cols = w_key.shape[1]
    cosine, sine = rope_tables(length)
    late = jax.ShapeDtypeStruct((4 * small, width - cut), BF16)
    one = jax.ShapeDtypeStruct((2 * small, cut // 2), BF16)
    early = jax.ShapeDtypeStruct((2 * small, cut), BF16)
    send, up_1, down_1, ordered = pl.pallas_call(
        text_kernel,
        out_shape=[late, one, one, jax.ShapeDtypeStruct((length, q_cols), BF16)],
        in_specs=[far] * 5 + [whole, far, far, whole],
        out_specs=[anywhere] * 4,
        scratch_shapes=[
            pltpu.VMEM((length, width), BF16),
            pltpu.VMEM((width, q_cols + 2 * kv_cols), BF16),
            pltpu.VMEM((q_cols, width), BF16),
            pltpu.VMEM((2, length, HD), F32),
            pltpu.VMEM((length, q_cols + 2 * kv_cols), F32),
            pltpu.VMEM((length, q_cols), BF16),
            pltpu.VMEM((length, kv_cols), BF16),
            pltpu.VMEM((length, 2 * kv_cols), BF16),
            pltpu.VMEM((length, q_cols), BF16),
            pltpu.VMEM((length, q_cols), BF16),
            pltpu.VMEM((2 * small, cut), BF16),
            pltpu.VMEM(late.shape, BF16),
            pltpu.SemaphoreType.DMA((5, 4)),
            pltpu.SemaphoreType.DMA((4,)),
        ],
        compiler_params=pltpu.CompilerParams(vmem_limit_bytes=56 * 1024 * 1024),
        name="text_tower",
    )(
        hidden, w_query, w_key, w_value, w_out, attn_gain.reshape(1, width),
        jnp.asarray(cosine), jnp.asarray(sine), segment_ids,
    )
    swapped = lax.ppermute(send, "mp", Z_SWAP)
    up_1 = lax.ppermute(up_1, "mp", y_shift(1))
    down_1 = lax.ppermute(down_1, "mp", y_shift(3))
    up_near, down_near, up_2, down_2, a_own, keep, lined = pl.pallas_call(
        rest_kernel,
        out_shape=[one] * 4 + [early, late, jax.ShapeDtypeStruct((DOCS_DEV, HD), BF16)],
        in_specs=[whole] * 5,
        out_specs=[whole] * 7,
        compiler_params=pltpu.CompilerParams(vmem_limit_bytes=24 * 1024 * 1024),
        cost_estimate=pl.CostEstimate(
            flops=length * q_cols * width, bytes_accessed=4 * q_cols * width, transcendentals=0
        ),
        name="other_terms",
    )(ordered, w_out, features, ln_gain.reshape(1, emb), ln_bias.reshape(1, emb))
    up_near = lax.ppermute(up_near, "mp", y_shift(1))
    down_near = lax.ppermute(down_near, "mp", y_shift(3))
    rows = lax.dynamic_slice_in_dim(hidden, mine * small, small, 0)
    up_2, rows = lax.optimization_barrier((up_2, rows))
    up_2, down_2 = pl.pallas_call(
        pass_on_kernel,
        out_shape=[one, one],
        in_specs=[whole] * 4,
        out_specs=[whole] * 2,
        compiler_params=params,
        name="pass_on",
    )(up_2, down_2, up_1, down_1)
    r_up = lax.ppermute(up_2, "mp", y_shift(1))
    r_down = lax.ppermute(down_2, "mp", y_shift(3))
    weights = pl.pallas_call(
        fetch_kernel,
        out_shape=jax.ShapeDtypeStruct(adapter.shape, BF16),
        in_specs=[anywhere] * 2,
        out_specs=whole,
        scratch_shapes=[pltpu.SemaphoreType.DMA],
        compiler_params=params,
        name="fetch_weights",
    )(adapter, up_2)
    blocks = pl.pallas_call(
        swap_kernel,
        out_shape=[jax.ShapeDtypeStruct((small, width - cut), BF16)] * 4,
        in_specs=[whole] * 2 + [anywhere],
        out_specs=[whole] * 4,
        compiler_params=params,
        name="add_swapped",
    )(keep, swapped, weights)
    q_2 = lax.ppermute(blocks[2], "mp", y_shift(2))
    q_1 = lax.ppermute(blocks[1], "mp", y_shift(1))
    q_3 = lax.ppermute(blocks[3], "mp", y_shift(3))
    kept, sent = pl.pallas_call(
        fold_kernel,
        out_shape=[
            jax.ShapeDtypeStruct((small, cut), F32),
            jax.ShapeDtypeStruct((small, cut), BF16),
        ],
        in_specs=[whole] * 5 + [anywhere],
        out_specs=[whole] * 2,
        compiler_params=params,
        name="fold",
    )(a_own, up_near, down_near, r_up, r_down, blocks[2])
    a_z = lax.ppermute(sent, "mp", Z_SWAP)
    seg = segment_ids[0]
    docs = jnp.arange(DOCS_DEV, dtype=jnp.int32)[:, None]
    counts = jnp.sum((docs == seg[None, :]).astype(F32), axis=1, keepdims=True)
    seg_rows = lax.dynamic_slice_in_dim(seg, mine * small, small, 0)
    member = (docs == seg_rows[None, :]).astype(F32) / counts
    own_cols = width // tensor_count
    chips = seqs // 2
    message = pl.pallas_call(
        pool_kernel,
        out_shape=jax.ShapeDtypeStruct((tensor_count, DOCS_DEV, emb + own_cols + HD), BF16),
        in_specs=[whole] * 11,
        out_specs=whole,
        scratch_shapes=[pltpu.VMEM((DOCS_DEV, width), BF16)],
        compiler_params=params,
        name="pool_and_project",
    )(
        rows, weights, member, final_gain.reshape(1, width), lined,
        kept, a_z, blocks[0], q_1, q_2, q_3,
    )
    message = lax.all_to_all(message, "mp", 0, 0, tiled=True)
    second = pl.pallas_call(
        sum_kernel,
        out_shape=jax.ShapeDtypeStruct((chips, DOCS_DEV, 2 * emb + HD), BF16),
        in_specs=[whole],
        out_specs=whole,
        scratch_shapes=[pltpu.VMEM((DOCS_DEV, emb), F32)],
        compiler_params=params,
        name="sum_partials",
    )(message)
    second = lax.all_to_all(
        second, "dp", 0, 0, tiled=True,
        axis_index_groups=[[2 * chip + core for chip in range(chips)] for core in range(2)],
    ).reshape(chips * DOCS_DEV, 2 * emb + HD)
    other = lax.ppermute(second, "dp", [(d, d ^ 1) for d in range(seqs)])
    count = seqs * DOCS_DEV
    own = width // (seqs * tensor_count)
    loss, adapter_grad, feature_grad = pl.pallas_call(
        loss_kernel,
        out_shape=[
            jax.ShapeDtypeStruct((1, 1), F32),
            jax.ShapeDtypeStruct((own, emb), F32),
            jax.ShapeDtypeStruct((emb_rows, emb), F32),
        ],
        in_specs=[whole] * 6,
        out_specs=[whole] * 3,
        scratch_shapes=[pltpu.VMEM((count, 2 * emb + HD), BF16), pltpu.VMEM((HD, emb), F32)],
        compiler_params=params,
        name="loss_and_gradients",
    )(
        second, other, features,
        ln_gain.reshape(1, emb), ln_bias.reshape(1, emb), pair_ids.reshape(1, count),
    )
    return (loss[0, 0], adapter_grad, feature_grad)


def solution(mesh):
    return jax.shard_map(
        on_device,
        mesh=mesh,
        in_specs=(
            P("dp", None),
            P("dp", None),
            P(),
            P(None, "mp"),
            P(None, "mp"),
            P(None, "mp"),
            P("mp", None),
            P(),
            P(),
            P(("dp", "mp"), None),
            P(),
            P(),
            P(),
        ),
        out_specs=(P(), P(("dp", "mp"), None), P(("dp", "mp"), None)),
        check_vma=False,
    )
```

```python
import jax
import jax.numpy as jnp
import numpy as np
from jax import lax
from jax.experimental import pallas as pl
from jax.experimental.pallas import tpu as pltpu
from jax.sharding import PartitionSpec as P

HD = 128
DOCS_DEV = 16
SCALE = 1.0 / 0.07
EPS = 1e-05
HIGH = lax.Precision.HIGHEST
F32 = jnp.float32
BF16 = jnp.bfloat16


def rope_tables(length):
    half = HD // 2
    freq = 500000.0 ** (-np.arange(half) * 2.0 / HD)
    angle = np.arange(length)[:, None] * freq[None, :]
    cosine = np.concatenate([np.cos(angle), np.cos(angle)], axis=1)
    sine = np.concatenate([-np.sin(angle), np.sin(angle)], axis=1)
    return cosine.astype(np.float32), sine.astype(np.float32)


def dot(left, right, precision=None):
    return jnp.dot(left, right, precision=precision, preferred_element_type=F32)


def dot_rows(left, right, precision=None):
    return lax.dot_general(
        left, right, (((1,), (1,)), ((), ())), precision=precision, preferred_element_type=F32
    )


def text_kernel(
    hidden, w_query, w_key, w_value, w_out, gain, cosine, sine, seg,
    z_send, up_1, down_1, ordered_out,
    hid, w_in, w_up, table, acc, query, keys, values, att, ordered, stage, stage_send, sems, out_sems,
):
    length, width = hidden.shape
    q_local = w_query.shape[1] // HD
    parts = 8
    span = width // parts
    q_cols = w_query.shape[1]
    kv_cols = w_key.shape[1]
    copies = []
    for part in range(parts):
        rows = pl.ds(part * span, span)
        group = [
            pltpu.make_async_copy(hidden.at[:, rows], hid.at[:, rows], sems.at[part, 0]),
            pltpu.make_async_copy(
                w_query.at[rows, :], w_in.at[rows, pl.ds(0, q_cols)], sems.at[part, 1]
            ),
            pltpu.make_async_copy(
                w_key.at[rows, :], w_in.at[rows, pl.ds(q_cols, kv_cols)], sems.at[part, 2]
            ),
            pltpu.make_async_copy(
                w_value.at[rows, :], w_in.at[rows, pl.ds(q_cols + kv_cols, kv_cols)], sems.at[part, 3]
            ),
        ]
        for copy in group:
            copy.start()
        copies.append(group)
    table_copies = [
        pltpu.make_async_copy(cosine, table.at[0], sems.at[parts, 1]),
        pltpu.make_async_copy(sine, table.at[1], sems.at[parts, 2]),
    ]
    for copy in table_copies:
        copy.start()
    up_copy = pltpu.make_async_copy(w_out, w_up, sems.at[parts, 0])
    up_copy.start()
    squares = jnp.zeros((length, HD), F32)
    for part in range(parts):
        for copy in copies[part]:
            copy.wait()
        cols = slice(part * span, (part + 1) * span)
        stream = hid[:, cols].astype(F32)
        for lane in range(0, span, HD):
            piece = stream[:, lane : lane + HD]
            squares = squares + piece * piece
        scaled = (stream * gain[:, cols]).astype(BF16)
        product = dot(scaled, w_in[cols, :])
        if part == 0:
            acc[...] = product
        else:
            acc[...] += product
    norm = lax.rsqrt(jnp.sum(squares, axis=1, keepdims=True) * (1.0 / width) + EPS)
    for copy in table_copies:
        copy.wait()
    cos_t = table[0] * norm
    sin_t = table[1] * norm
    value = acc[:, q_cols : q_cols + HD]
    keys[...] = (value * cos_t + pltpu.roll(value, HD // 2, 1) * sin_t).astype(BF16)
    values[:, 0:HD] = (acc[:, q_cols + HD :] * norm).astype(BF16)
    values[:, HD:] = jnp.ones((length, HD), BF16)
    cos_t = cos_t * HD ** (-0.5)
    sin_t = sin_t * HD ** (-0.5)
    for head in range(q_local):
        lanes = slice(head * HD, (head + 1) * HD)
        value = acc[:, lanes]
        query[:, lanes] = (value * cos_t + pltpu.roll(value, HD // 2, 1) * sin_t).astype(BF16)
    block = 128
    seg_f = seg[...].astype(F32)
    for at in range(length // block):
        first = max(0, at - 1) * block
        last = (at + 1) * block
        rows = slice(at * block, last)
        seg_q = jnp.broadcast_to(seg_f[:, rows], (block, block)).T
        masks = []
        for key_at in range(first, last, block):
            seg_k = jnp.broadcast_to(seg_f[:, key_at : key_at + block], (block, block))
            live = seg_q == seg_k
            if key_at == at * block:
                live = live & (
                    lax.broadcasted_iota(jnp.int32, (block, block), 0)
                    >= lax.broadcasted_iota(jnp.int32, (block, block), 1)
                )
            masks.append(jnp.where(live, 0.0, -1e30))
        mask = masks[0] if len(masks) == 1 else jnp.concatenate(masks, axis=1)
        mask = jnp.concatenate([mask] * q_local, axis=0)
        stacked = jnp.concatenate(
            [query[rows, head * HD : (head + 1) * HD] for head in range(q_local)], axis=0
        )
        score = dot_rows(stacked, keys[first:last, :]) + mask
        weight = jnp.exp(score - jnp.max(score, axis=1, keepdims=True)).astype(BF16)
        result = dot(weight, values[first:last, :])
        result = (result[:, 0:HD] / result[:, HD:]).astype(BF16)
        for head in range(q_local):
            att[rows, head * HD : (head + 1) * HD] = result[head * block : (head + 1) * block]
    index = lax.axis_index("mp")
    y, z = index // 2, lax.rem(index, 2)
    small = length // 8
    for step in range(4):
        base = lax.rem(y + step, 4) * 2
        mine = pl.multiple_of((base + z) * small, small)
        other = pl.multiple_of((base + 1 - z) * small, small)
        at = step * small
        ordered[pl.ds(at, small), :] = att[pl.ds(mine, small), :]
        ordered[pl.ds(4 * small + at, small), :] = att[pl.ds(other, small), :]
    up_copy.wait()
    side = up_1.shape[1]
    cut = 2 * side
    sends = []

    def ship(source, target):
        send = pltpu.make_async_copy(source, target, out_sems.at[len(sends)])
        send.start()
        sends.append(send)

    for start, stop in pieces(cut, width):
        stage_send[:, start - cut : stop - cut] = dot(
            ordered[4 * small :, :], w_up[:, start:stop]
        ).astype(BF16)
    ship(stage_send, z_send)
    ship(ordered, ordered_out)
    far = jnp.concatenate(
        [ordered[2 * small : 3 * small, :], ordered[6 * small : 7 * small, :]], axis=0
    )
    for start, stop in pieces(0, cut):
        stage[:, start:stop] = dot(far, w_up[:, start:stop]).astype(BF16)
    ship(stage.at[:, pl.ds(0, side)], up_1)
    ship(stage.at[:, pl.ds(side, side)], down_1)
    for send in sends:
        send.wait()


def pieces(first, last, chunk=512):
    edges = list(range(first, last - chunk + 1, chunk)) + [last]
    return list(zip(edges[:-1], edges[1:]))


def rest_kernel(ordered, w_out, up_near, down_near, up_2, down_2, own, keep):
    side = up_2.shape[1]
    cut = 2 * side
    width = w_out.shape[1]
    small = keep.shape[0] // 4
    wide = 2 * small
    rows = jnp.concatenate(
        [
            ordered[(4 * half + step) * small : (4 * half + step + 1) * small, :]
            for step in (1, 3, 0)
            for half in range(2)
        ],
        axis=0,
    )
    for base, near, far in ((0, (down_near, 1), (up_2, 0)), (side, (up_near, 0), (down_2, 1))):
        for start, stop in pieces(base, base + side):
            result = dot(rows, w_out[:, start:stop]).astype(BF16)
            cols = slice(start - base, stop - base)
            for ref, at in (near, far):
                ref[:, cols] = result[at * wide : (at + 1) * wide]
            own[:, start:stop] = result[2 * wide :]
    for start, stop in pieces(cut, width):
        keep[:, start - cut : stop - cut] = dot(
            ordered[0 : 4 * small, :], w_out[:, start:stop]
        ).astype(BF16)


def add(left, right):
    return (left.astype(F32) + right.astype(F32)).astype(BF16)


def pass_on_kernel(up_2, down_2, up_1, down_1, up, down):
    up[...] = add(up_2[...], up_1[...])
    down[...] = add(down_2[...], down_1[...])


def swap_kernel(keep, swapped, after, block_0, block_1, block_2, block_3):
    size = block_0.shape[0]
    for step, block in enumerate((block_0, block_1, block_2, block_3)):
        rows = slice(step * size, (step + 1) * size)
        block[...] = add(keep[rows, :], swapped[rows, :])


def fold_kernel(own, up_near, down_near, up_2, down_2, after, kept, sent):
    small = kept.shape[0]
    total = ring_sum(own, up_near, down_near, up_2, down_2)
    kept[...] = total[:small]
    sent[...] = total[small:].astype(BF16)


def fetch_kernel(adapter, after, weights, sem):
    copy = pltpu.make_async_copy(adapter, weights, sem)
    copy.start()
    copy.wait()


def ring_sum(own, up_near, down_near, up_2, down_2):
    width = own.shape[1]
    side = width // 2
    left = own[:, 0:side].astype(F32) + down_near[...].astype(F32) + up_2[...].astype(F32)
    right = own[:, side:].astype(F32) + up_near[...].astype(F32) + down_2[...].astype(F32)
    return jnp.concatenate([left, right], axis=1)


def pool_kernel(
    rows, adapter, member, gain, features, kept, a_z, b_own, b_1, b_2, b_3, message, doc,
):
    small, width = rows.shape
    left = kept[...] + a_z[...].astype(F32)
    right = b_own[...].astype(F32) + b_1[...].astype(F32)
    right = right + b_2[...].astype(F32) + b_3[...].astype(F32)
    residual = jnp.concatenate([left, right], axis=1) + rows[...].astype(F32)
    norm = lax.rsqrt(jnp.sum(residual * residual, axis=1, keepdims=True) * (1.0 / width) + EPS)
    final = residual * norm * gain[...]
    means = dot(member[...], final, HIGH)
    doc[...] = means.astype(BF16)
    emb = adapter.shape[1]
    projected = dot(doc[...], adapter[...])
    projected = projected.astype(BF16)
    own = 32
    seqs = 16
    lane = lax.broadcasted_iota(jnp.int32, (DOCS_DEV, HD), 1) // own
    for peer in range(8):
        message[peer, :, 0:emb] = projected
        for group in range(seqs // 4):
            tile = None
            for slot in range(4):
                at = (2 * (group * 4 + slot) + peer // 4) * HD
                piece = means[:, at : at + HD]
                shift = ((slot - peer % 4) * own) % HD
                if shift:
                    piece = pltpu.roll(piece, shift, 1)
                tile = piece if tile is None else jnp.where(lane == slot, piece, tile)
            message[peer, :, emb + group * HD : emb + (group + 1) * HD] = tile.astype(BF16)
    image_rows = features[...].astype(F32)
    per_row = emb // HD
    lined = jnp.concatenate(
        [
            image_rows[row : row + 1, at * HD : (at + 1) * HD]
            for row in range(features.shape[0])
            for at in range(per_row)
        ],
        axis=0,
    ).astype(BF16)
    for peer in range(8):
        message[peer, :, emb + seqs * own :] = lined


def sum_kernel(message, second, images):
    emb = images.shape[1]
    cut = message.shape[2] - HD
    total = message[0, :, 0:cut].astype(F32)
    for peer in range(1, message.shape[0]):
        total = total + message[peer, :, 0:cut].astype(F32)
    total = total.astype(BF16)
    per_row = emb // HD
    for peer in range(message.shape[0]):
        lined = message[peer, :, cut:].astype(F32)
        for at in range(lined.shape[0]):
            row = peer * (lined.shape[0] // per_row) + at // per_row
            lane = (at % per_row) * HD
            images[row : row + 1, lane : lane + HD] = lined[at : at + 1, :]
    image_rows = images[...].astype(BF16)
    for chip in range(second.shape[0]):
        second[chip, :, 0:emb] = total[:, 0:emb]
        at = emb + (chip // 2) * HD
        second[chip, :, emb : emb + HD] = total[:, at : at + HD]
        second[chip, :, emb + HD :] = image_rows


def image_tower(values, gain, shift):
    center = values - jnp.mean(values, axis=1, keepdims=True)
    spread = lax.rsqrt(jnp.mean(center * center, axis=1, keepdims=True) + EPS)
    unit = center * spread
    normal = unit * gain + shift
    scale = lax.rsqrt(jnp.sum(normal * normal, axis=1, keepdims=True) + 1e-06)
    return unit, spread, normal * scale, scale


def split(value):
    high = value.astype(BF16)
    return high, (value - high.astype(F32)).astype(BF16)


def loss_kernel(
    same, other, features, ln_gain, ln_bias, pairs, loss, adapter_grad, feature_grad, all_rows, wide
):
    count = all_rows.shape[0]
    emb = features.shape[1]
    core = lax.rem(lax.axis_index("dp"), 2)
    for chip in range(count // (2 * DOCS_DEV)):
        rows = slice(chip * DOCS_DEV, (chip + 1) * DOCS_DEV)
        for ref, at in ((same, core), (other, 1 - core)):
            start = pl.multiple_of((2 * chip + at) * DOCS_DEV, DOCS_DEV)
            all_rows[pl.ds(start, DOCS_DEV), :] = ref[rows, :]
    image = image_tower(all_rows[:, emb + HD :].astype(F32), ln_gain[...], ln_bias[...])[2]
    image_high, image_low = split(image)
    narrow = all_rows[:, 0:emb]
    projected = narrow.astype(F32)
    text_scale = lax.rsqrt(jnp.sum(projected * projected, axis=1, keepdims=True) + 1e-06)
    text = projected * text_scale
    scores = (SCALE * text_scale) * (dot_rows(narrow, image_high) + dot_rows(narrow, image_low))
    grown = jnp.exp(scores)
    text_sum = jnp.sum(grown, axis=1, keepdims=True)
    image_sum = jnp.sum(grown, axis=0, keepdims=True)
    match = (lax.broadcasted_iota(jnp.int32, (count, count), 0) == pairs[...]).astype(F32)
    loss[...] = (
        jnp.sum(jnp.log(text_sum), axis=0, keepdims=True)
        + jnp.sum(jnp.log(image_sum), axis=1, keepdims=True)
        - 2.0 * jnp.sum(jnp.sum(scores * match, axis=1, keepdims=True), axis=0, keepdims=True)
    ) * (1.0 / (2.0 * count))
    dual = 0.5 * grown * (1.0 / text_sum + 1.0 / image_sum) - match
    dual_high, dual_low = split(dual)
    grad_text = SCALE * (
        dot(dual_high, image_high) + dot(dual_high, image_low) + dot(dual_low, image_high)
    )
    grad_projected = text_scale * (
        grad_text - text * jnp.sum(grad_text * text, axis=1, keepdims=True)
    )
    grad_high, grad_low = split(grad_projected)
    pooled = all_rows[:, emb : emb + HD].astype(F32).T.astype(BF16)
    wide[...] = dot(pooled, grad_high) + dot(pooled, grad_low)
    own = adapter_grad.shape[0]
    slot = pl.multiple_of(lax.rem(lax.axis_index("dp"), 4) * own, own)
    adapter_grad[...] = wide[pl.ds(slot, own), :]
    few = features.shape[0]
    chosen = (
        lax.broadcasted_iota(jnp.int32, (few, count), 1)
        == lax.axis_index(("dp", "mp")) * few + lax.broadcasted_iota(jnp.int32, (few, count), 0)
    ).astype(BF16)
    dual_own = dot_rows(chosen, dual_high) + dot_rows(chosen, dual_low)
    own_high, own_low = split(dual_own)
    text_high, text_low = split(text)
    grad_image = SCALE * (
        dot(own_high, text_high) + dot(own_high, text_low) + dot(own_low, text_high)
    )
    unit, spread, mine, scale = image_tower(
        features[...].astype(F32), ln_gain[...], ln_bias[...]
    )
    grad_normal = scale * (grad_image - mine * jnp.sum(grad_image * mine, axis=1, keepdims=True))
    grad_unit = grad_normal * ln_gain[...]
    feature_grad[...] = spread * (
        grad_unit
        - jnp.mean(grad_unit, axis=1, keepdims=True)
        - unit * jnp.mean(grad_unit * unit, axis=1, keepdims=True)
    )


def y_shift(step):
    return [(y * 2 + z, ((y + step) % 4) * 2 + z) for y in range(4) for z in range(2)]


Z_SWAP = [(m, m ^ 1) for m in range(8)]


def on_device(
    hidden,
    segment_ids,
    attn_gain,
    w_query,
    w_key,
    w_value,
    w_out,
    final_gain,
    adapter,
    features,
    ln_gain,
    ln_bias,
    pair_ids,
):
    length, width = hidden.shape
    emb_rows, emb = features.shape
    tensor_count = lax.axis_size("mp")
    seqs = lax.axis_size("dp")
    mine = lax.axis_index("mp")
    params = pltpu.CompilerParams(vmem_limit_bytes=16 * 1024 * 1024)
    roomy = pltpu.CompilerParams(vmem_limit_bytes=56 * 1024 * 1024)
    whole = pl.BlockSpec(memory_space=pltpu.VMEM)
    anywhere = pl.BlockSpec(memory_space=pl.ANY)
    far = pl.BlockSpec(memory_space=pltpu.HBM)
    small = length // 8
    cut = 2304
    q_cols = w_query.shape[1]
    kv_cols = w_key.shape[1]
    cosine, sine = rope_tables(length)
    late = jax.ShapeDtypeStruct((4 * small, width - cut), BF16)
    one = jax.ShapeDtypeStruct((2 * small, cut // 2), BF16)
    early = jax.ShapeDtypeStruct((2 * small, cut), BF16)
    send, up_1, down_1, ordered = pl.pallas_call(
        text_kernel,
        out_shape=[late, one, one, jax.ShapeDtypeStruct((length, q_cols), BF16)],
        in_specs=[far] * 5 + [whole, far, far, whole],
        out_specs=[anywhere] * 4,
        scratch_shapes=[
            pltpu.VMEM((length, width), BF16),
            pltpu.VMEM((width, q_cols + 2 * kv_cols), BF16),
            pltpu.VMEM((q_cols, width), BF16),
            pltpu.VMEM((2, length, HD), F32),
            pltpu.VMEM((length, q_cols + 2 * kv_cols), F32),
            pltpu.VMEM((length, q_cols), BF16),
            pltpu.VMEM((length, kv_cols), BF16),
            pltpu.VMEM((length, 2 * kv_cols), BF16),
            pltpu.VMEM((length, q_cols), BF16),
            pltpu.VMEM((length, q_cols), BF16),
            pltpu.VMEM((2 * small, cut), BF16),
            pltpu.VMEM(late.shape, BF16),
            pltpu.SemaphoreType.DMA((9, 4)),
            pltpu.SemaphoreType.DMA((4,)),
        ],
        compiler_params=pltpu.CompilerParams(vmem_limit_bytes=56 * 1024 * 1024),
        name="text_tower",
    )(
        hidden, w_query, w_key, w_value, w_out, attn_gain.reshape(1, width),
        jnp.asarray(cosine), jnp.asarray(sine), segment_ids,
    )
    swapped = lax.ppermute(send, "mp", Z_SWAP)
    up_1 = lax.ppermute(up_1, "mp", y_shift(1))
    down_1 = lax.ppermute(down_1, "mp", y_shift(3))
    up_near, down_near, up_2, down_2, a_own, keep = pl.pallas_call(
        rest_kernel,
        out_shape=[one] * 4 + [early, late],
        in_specs=[whole] * 2,
        out_specs=[whole] * 6,
        compiler_params=pltpu.CompilerParams(vmem_limit_bytes=24 * 1024 * 1024),
        cost_estimate=pl.CostEstimate(
            flops=length * q_cols * width, bytes_accessed=4 * q_cols * width, transcendentals=0
        ),
        name="other_terms",
    )(ordered, w_out)
    up_near = lax.ppermute(up_near, "mp", y_shift(1))
    down_near = lax.ppermute(down_near, "mp", y_shift(3))
    rows = lax.dynamic_slice_in_dim(hidden, mine * small, small, 0)
    up_2, rows = lax.optimization_barrier((up_2, rows))
    up_2, down_2 = pl.pallas_call(
        pass_on_kernel,
        out_shape=[one, one],
        in_specs=[whole] * 4,
        out_specs=[whole] * 2,
        compiler_params=params,
        name="pass_on",
    )(up_2, down_2, up_1, down_1)
    r_up = lax.ppermute(up_2, "mp", y_shift(1))
    r_down = lax.ppermute(down_2, "mp", y_shift(3))
    weights = pl.pallas_call(
        fetch_kernel,
        out_shape=jax.ShapeDtypeStruct(adapter.shape, BF16),
        in_specs=[anywhere] * 2,
        out_specs=whole,
        scratch_shapes=[pltpu.SemaphoreType.DMA],
        compiler_params=params,
        name="fetch_weights",
    )(adapter, up_2)
    blocks = pl.pallas_call(
        swap_kernel,
        out_shape=[jax.ShapeDtypeStruct((small, width - cut), BF16)] * 4,
        in_specs=[whole] * 2 + [anywhere],
        out_specs=[whole] * 4,
        compiler_params=params,
        name="add_swapped",
    )(keep, swapped, weights)
    q_2 = lax.ppermute(blocks[2], "mp", y_shift(2))
    q_1 = lax.ppermute(blocks[1], "mp", y_shift(1))
    q_3 = lax.ppermute(blocks[3], "mp", y_shift(3))
    kept, sent = pl.pallas_call(
        fold_kernel,
        out_shape=[
            jax.ShapeDtypeStruct((small, cut), F32),
            jax.ShapeDtypeStruct((small, cut), BF16),
        ],
        in_specs=[whole] * 5 + [anywhere],
        out_specs=[whole] * 2,
        compiler_params=params,
        name="fold",
    )(a_own, up_near, down_near, r_up, r_down, blocks[2])
    a_z = lax.ppermute(sent, "mp", Z_SWAP)
    seg = segment_ids[0]
    docs = jnp.arange(DOCS_DEV, dtype=jnp.int32)[:, None]
    counts = jnp.sum((docs == seg[None, :]).astype(F32), axis=1, keepdims=True)
    seg_rows = lax.dynamic_slice_in_dim(seg, mine * small, small, 0)
    member = (docs == seg_rows[None, :]).astype(F32) / counts
    own_cols = width // tensor_count
    chips = seqs // 2
    message = pl.pallas_call(
        pool_kernel,
        out_shape=jax.ShapeDtypeStruct((tensor_count, DOCS_DEV, emb + own_cols + HD), BF16),
        in_specs=[whole] * 11,
        out_specs=whole,
        scratch_shapes=[pltpu.VMEM((DOCS_DEV, width), BF16)],
        compiler_params=params,
        name="pool_and_project",
    )(
        rows, weights, member, final_gain.reshape(1, width), features,
        kept, a_z, blocks[0], q_1, q_2, q_3,
    )
    message = lax.all_to_all(message, "mp", 0, 0, tiled=True)
    second = pl.pallas_call(
        sum_kernel,
        out_shape=jax.ShapeDtypeStruct((chips, DOCS_DEV, 2 * emb + HD), BF16),
        in_specs=[whole],
        out_specs=whole,
        scratch_shapes=[pltpu.VMEM((DOCS_DEV, emb), F32)],
        compiler_params=params,
        name="sum_partials",
    )(message)
    second = lax.all_to_all(
        second, "dp", 0, 0, tiled=True,
        axis_index_groups=[[2 * chip + core for chip in range(chips)] for core in range(2)],
    ).reshape(chips * DOCS_DEV, 2 * emb + HD)
    other = lax.ppermute(second, "dp", [(d, d ^ 1) for d in range(seqs)])
    count = seqs * DOCS_DEV
    own = width // (seqs * tensor_count)
    loss, adapter_grad, feature_grad = pl.pallas_call(
        loss_kernel,
        out_shape=[
            jax.ShapeDtypeStruct((1, 1), F32),
            jax.ShapeDtypeStruct((own, emb), F32),
            jax.ShapeDtypeStruct((emb_rows, emb), F32),
        ],
        in_specs=[whole] * 6,
        out_specs=[whole] * 3,
        scratch_shapes=[pltpu.VMEM((count, 2 * emb + HD), BF16), pltpu.VMEM((HD, emb), F32)],
        compiler_params=params,
        name="loss_and_gradients",
    )(
        second, other, features,
        ln_gain.reshape(1, emb), ln_bias.reshape(1, emb), pair_ids.reshape(1, count),
    )
    return (loss[0, 0], adapter_grad, feature_grad)


def solution(mesh):
    return jax.shard_map(
        on_device,
        mesh=mesh,
        in_specs=(
            P("dp", None),
            P("dp", None),
            P(),
            P(None, "mp"),
            P(None, "mp"),
            P(None, "mp"),
            P("mp", None),
            P(),
            P(),
            P(("dp", "mp"), None),
            P(),
            P(),
            P(),
        ),
        out_specs=(P(), P(("dp", "mp"), None), P(("dp", "mp"), None)),
        check_vma=False,
    )
```
